32 devices in a mesh: dp: 8 (over y, x, core), expert: 4 (over z).
Axes of the slice: x: 2, y: 2, z: 4, core: 2. Of those that a mesh axis runs over, the one named last changes fastest.
Arguments:
- expert_partials: float32 [8, 4, 1536, 2048], P('dp', 'expert'), may hold values from -5 to 5
- key_partials: float32 [8, 512, 4096], P('dp', None, 'expert'), may hold values from -5 to 5
- expert_param: float32 [4, 1536, 2048], P('expert', 'dp'), may hold values from -0.3125 to 0.3125
- expert_moment: float32 [4, 1536, 2048], P('expert', 'dp'), may hold values from -4 to 4
- expert_second: float32 [4, 1536, 2048], P('expert', 'dp'), may hold values from 0.05 to 1
- key_param: float32 [512, 4096], P('dp', 'expert'), may hold values from -0.3125 to 0.3125
- key_moment: float32 [512, 4096], P('dp', 'expert'), may hold values from -4 to 4
- key_second: float32 [512, 4096], P('dp', 'expert'), may hold values from 0.05 to 1
- expert_scales: float32 [4, 12, 16], replicated, may hold values from 0.0001 to 0.001
- key_scales: float32 [4, 32], P(None, 'expert'), may hold values from 0.0001 to 0.001
- rotary_order: int32 [128], replicated, may hold values from 0 to 127, each once
- expert_slot: int32 [4], replicated, may hold values from 0 to 3, each once
Outputs:
- new_expert_param: float32 [4, 1536, 2048], P('expert', 'dp')
- new_expert_moment: float32 [4, 1536, 2048], P('expert', 'dp')
- new_expert_second: float32 [4, 1536, 2048], P('expert', 'dp')
- new_key_param: float32 [512, 4096], P('dp', 'expert')
- new_key_moment: float32 [512, 4096], P('dp', 'expert')
- new_key_second: float32 [512, 4096], P('dp', 'expert')
- server_expert: bfloat16 [4, 2048, 1536], P(None, 'expert', 'dp')
- server_key: bfloat16 [4096, 512], P('expert')
The draws below stay inside these ranges and needn't reach their ends.
Inputs may be any that keep to these rules, and one draw needn't show every extreme that they name: `rotary_order`: a permutation of the rows of one head. `expert_slot`: a permutation of the experts.
All inputs are finite; a program needn't handle non-finite values.
Results may differ from the reference program's by a relative error of at most 0.007.
Values may be sent and summed in bfloat16 or wider, within the bound.
A program may use at most 128 MiB of HBM per device.

```python
import math
import jax
import jax.numpy as jnp
from jax import lax

D = 4096
DW = 2048
FW = 1536
HD = 128
BLOCK = 128
EXPERTS = 4
KR = 512
N_DP = 8


def strengthened(values, rng, source, target, parts, factor):
    def block_of(dim):
        return (jnp.arange(values.shape[dim]) // (values.shape[dim] // parts)).reshape((-1,) + (1,) * (values.ndim - 1 - dim))

    near = jax.random.permutation(rng, parts)[block_of(target)]
    second = (block_of(target) + parts // 2) % parts
    return jnp.where((block_of(source) == near) | (block_of(source) == second), factor * values, values)


def block_levels(own_key, dims, shards, smallest, high):
    gain = 1.0
    for position, blocks in shards:
        draws = jax.random.uniform(jax.random.fold_in(jax.random.fold_in(own_key, 6), position), (blocks,), jnp.float32, smallest / len(shards), high / len(shards))
        gain = gain * jnp.repeat(jnp.exp(draws), dims[position] // blocks).reshape((-1,) + (1,) * (len(dims) - 1 - position))
    return gain


def normal_values(stream_key, shape, spread, limit, shards=(), held_as=jnp.bfloat16):
    array = spread * jax.random.normal(stream_key, shape, jnp.float32)
    if shards:
        array = array * block_levels(stream_key, shape, shards, -0.22, 0.18)
    return jnp.clip(array, -limit, limit).astype(held_as)


def noise_with(key, extent, spread, bound, split, heavy, kind=jnp.bfloat16):
    result = spread * jax.random.normal(key, extent, jnp.float32)
    if split:
        result = result * block_levels(key, extent, split, -0.22, 0.18)
    return jnp.clip(strengthened(result, jax.random.fold_in(key, 3), *heavy), -bound, bound).astype(kind)


def setup_inputs(seed: int = 0) -> dict:
    arg_keys = jax.random.split(jax.random.key(seed), 13)
    expert_partials = noise_with(arg_keys[0], (N_DP, EXPERTS, FW, DW), 0.25, 5.0, ((0, 8), (1, 4)), (0, 2, 8, 2.0), jnp.float32)
    key_partials = noise_with(arg_keys[1], (N_DP, KR, D), 0.25, 5.0, ((0, 8), (2, 4)), (0, 1, 8, 2.0), jnp.float32)
    expert_param = normal_values(arg_keys[2], (EXPERTS, FW, DW), 0.02, 0.3125, ((0, 4), (1, 8)), jnp.float32)
    expert_moment = normal_values(arg_keys[3], (EXPERTS, FW, DW), 0.3, 4.0, ((0, 4), (1, 8)), jnp.float32)
    expert_second = jnp.clip(jnp.exp(math.log(1.0) - 2.9957323 * jax.random.uniform(arg_keys[4], (EXPERTS, FW, DW), jnp.float32) ** block_levels(arg_keys[4], (EXPERTS, FW, DW), ((0, 4), (1, 8)), -0.2, 0.2)), 0.05, 1.0)
    key_param = normal_values(arg_keys[5], (KR, D), 0.02, 0.3125, ((0, 8), (1, 4)), jnp.float32)
    key_moment = normal_values(arg_keys[6], (KR, D), 0.3, 4.0, ((0, 8), (1, 4)), jnp.float32)
    key_second = jnp.clip(jnp.exp(math.log(1.0) - 2.9957323 * jax.random.uniform(arg_keys[7], (KR, D), jnp.float32) ** block_levels(arg_keys[7], (KR, D), ((0, 8), (1, 4)), -0.2, 0.2)), 0.05, 1.0)
    expert_scales = jnp.clip(jnp.exp(jax.random.uniform(arg_keys[8], (EXPERTS, FW // BLOCK, DW // BLOCK), jnp.float32, math.log(0.0001), math.log(0.001))), 0.0001, 0.001)
    key_scales = jnp.clip(jnp.exp(math.log(0.001) - 2.3025852 * jax.random.uniform(arg_keys[9], (KR // BLOCK, D // BLOCK), jnp.float32) ** block_levels(arg_keys[9], (KR // BLOCK, D // BLOCK), ((1, 4),), -0.2, 0.2)), 0.0001, 0.001)
    rotary_order = jax.random.permutation(arg_keys[10], HD).astype(jnp.int32)
    expert_slot = jax.random.permutation(arg_keys[11], EXPERTS).astype(jnp.int32)
    return {"expert_partials": expert_partials, "key_partials": key_partials, "expert_param": expert_param, "expert_moment": expert_moment, "expert_second": expert_second, "key_param": key_param, "key_moment": key_moment, "key_second": key_second, "expert_scales": expert_scales, "key_scales": key_scales, "rotary_order": rotary_order, "expert_slot": expert_slot}


BETA_ONE = 0.9
BETA_TWO = 0.95
LEARN = 0.01
DECAY = 0.1
EPSILON = 1e-08
LIMIT = 448.0
CORRECT_ONE = 1.0 - 0.9 ** 10
CORRECT_TWO = 1.0 - 0.95 ** 10

def adam_update(param, moment, second, grad):
    moment = BETA_ONE * moment + (1.0 - BETA_ONE) * grad
    second = BETA_TWO * second + (1.0 - BETA_TWO) * grad * grad
    corrected = moment / CORRECT_ONE / (jnp.sqrt(second / CORRECT_TWO) + EPSILON)
    return (param * (1.0 - LEARN * DECAY) - LEARN * corrected, moment, second)

def to_grid(weights, scales):
    return jnp.clip(weights / scales, -LIMIT, LIMIT).astype(jnp.bfloat16)

def reference(expert_partials, key_partials, expert_param, expert_moment, expert_second, key_param, key_moment, key_second, expert_scales, key_scales, rotary_order, expert_slot):
    expert_grad = lax.optimization_barrier(jnp.sum(expert_partials, axis=0))
    key_grad = lax.optimization_barrier(jnp.sum(key_partials, axis=0))
    new_ep, new_em, new_es = adam_update(expert_param, expert_moment, expert_second, expert_grad)
    new_kp, new_km, new_ks = adam_update(key_param, key_moment, key_second, key_grad)
    full_expert = jnp.repeat(jnp.repeat(expert_scales, BLOCK, axis=1), BLOCK, axis=2)
    expert_grid = to_grid(new_ep, full_expert)
    server_expert = jnp.zeros((EXPERTS, DW, FW), jnp.bfloat16).at[expert_slot].set(jnp.transpose(expert_grid, (0, 2, 1)))
    full_key = jnp.repeat(jnp.repeat(key_scales, BLOCK, axis=0), BLOCK, axis=1)
    key_grid = to_grid(new_kp, full_key)
    rows = jnp.arange(KR, dtype=jnp.int32)
    source = rows // HD * HD + rotary_order[rows % HD]
    server_key = jnp.take(key_grid, source, axis=0).T
    return (new_ep, new_em, new_es, new_kp, new_km, new_ks, server_expert, server_key)
```

```python
import functools
import math

import jax
import jax.numpy as jnp
from jax import lax
from jax.experimental import pallas as pl
from jax.experimental.pallas import tpu as pltpu
from jax.sharding import PartitionSpec as P

HD = 128
BLOCK = 128
BETA_ONE = 0.9
BETA_TWO = 0.95
LEARN = 0.01
DECAY = 0.1
EPSILON = 1e-08
LIMIT = 448.0
CORRECT_ONE = 1.0 - 0.9**10
CORRECT_TWO = 1.0 - 0.95**10
MESH = pl.DeviceIdType.MESH
F32 = jnp.float32
BF16 = jnp.bfloat16


def adam_update(param, moment, second, grad):
    moment = BETA_ONE * moment + (1.0 - BETA_ONE) * grad
    second = BETA_TWO * second + (1.0 - BETA_TWO) * grad * grad
    scaled = moment * (1.0 / CORRECT_ONE)
    corrected = scaled / (jnp.sqrt(second * (1.0 / CORRECT_TWO)) + EPSILON)
    return (param * (1.0 - LEARN * DECAY) - LEARN * corrected, moment, second)


def loop(count, body):
    def step(i, carry):
        body(i)
        return carry

    lax.fori_loop(0, count, step, 0)


def kernel(
    n_dp,
    n_ex,
    eg_hbm,
    kg_hbm,
    ep_hbm,
    em_hbm,
    es_hbm,
    kp_hbm,
    km_hbm,
    ks_hbm,
    e_scale,
    k_scale,
    order,
    o_ep,
    o_em,
    o_es,
    o_kp,
    o_km,
    o_ks,
    o_arr,
    o_key,
    e_far,
    e_own,
    e_s0s,
    e_s0r,
    e_state,
    e_grid,
    k_far,
    k_own,
    k_s0s,
    k_s0r,
    k_state,
    k_gath,
    k_out,
    *rest,
):
    chips = n_dp // 2
    m = chips.bit_length() - 1
    rest = list(rest)
    e_snd = [rest.pop(0) for _ in range(m)]
    e_rcv = [rest.pop(0) for _ in range(m)]
    k_snd = [rest.pop(0) for _ in range(m)]
    k_rcv = [rest.pop(0) for _ in range(m)]
    load_sem, s0_sem, rs_sem, out_sem, a2a_sem, ag_sem, pair_sem, key_sem = rest

    d = lax.axis_index("dp")
    z = lax.axis_index("expert")
    core = d % 2
    chip = d // 2
    bits = [(chip // 2**i) % 2 for i in range(m)]

    def chip_of(values):
        total = values[0] * 1
        for i in range(1, m):
            total = total + values[i] * 2**i
        return total

    def partner(i):
        return d + (1 - 2 * bits[i]) * 2 ** (i + 1)

    other_core = d + 1 - 2 * core
    orders = (list(range(m)), list(range(m))[::-1])

    rows, width = ep_hbm.shape[1:]
    krows, kwidth = kp_hbm.shape
    cw = width // n_ex

    def place(t):
        return (z + n_ex - 1 - t) % n_ex

    class Unit:
        pass

    units = []
    for u in range(n_ex + 1):
        w = Unit()
        w.u = u
        if u == 0:
            w.rows, w.cols = krows, kwidth
            w.columns = pl.ds(0, kwidth)
            w.far, w.own, w.s0s, w.s0r = k_far, k_own, k_s0s, k_s0r
            w.snd, w.rcv = k_snd, k_rcv
            w.grad = kg_hbm
            w.state = [k_state.at[i] for i in range(3)]
            w.state_in = [kp_hbm, km_hbm, ks_hbm]
            w.state_out = [o_kp, o_km, o_ks]
        else:
            t = u - 1
            w.dest = place(t)
            w.rows, w.cols = rows, cw
            w.columns = pl.ds(pl.multiple_of(w.dest * cw, cw), cw)
            w.far, w.own, w.s0s, w.s0r = (r.at[t] for r in (e_far, e_own, e_s0s, e_s0r))
            w.snd = [r.at[t] for r in e_snd]
            w.rcv = [r.at[t] for r in e_rcv]
            w.grad = eg_hbm
            w.state = [e_state.at[t, i] for i in range(3)]
            w.state_in = [r.at[0, :, w.columns] for r in (ep_hbm, em_hbm, es_hbm)]
            w.state_out = [r.at[0, :, w.columns] for r in (o_ep, o_em, o_es)]
        w.half = w.cols // 2
        w.load_far = pltpu.make_async_copy(
            w.grad.at[:, 1 - core, :, w.columns], w.far, load_sem.at[u, 0]
        )
        w.load_own = pltpu.make_async_copy(
            w.grad.at[:, core, :, w.columns], w.own, load_sem.at[u, 1]
        )
        w.load_state = [
            pltpu.make_async_copy(w.state_in[i], w.state[i], load_sem.at[u, 2 + i])
            for i in range(3)
        ]
        w.store_state = [
            pltpu.make_async_copy(w.state[i], w.state_out[i], out_sem.at[u, i])
            for i in range(3)
        ]
        w.s0 = pltpu.make_async_remote_copy(
            src_ref=w.s0s,
            dst_ref=w.s0r,
            send_sem=s0_sem.at[u, 0],
            recv_sem=s0_sem.at[u, 1],
            device_id=(other_core, z),
            device_id_type=MESH,
        )
        w.rs = [
            [
                pltpu.make_async_remote_copy(
                    src_ref=w.snd[s].at[h],
                    dst_ref=w.rcv[s].at[h],
                    send_sem=rs_sem.at[u, s, h, 0],
                    recv_sem=rs_sem.at[u, s, h, 1],
                    device_id=(partner(orders[h][s]), z),
                    device_id_type=MESH,
                )
                for h in range(2)
            ]
            for s in range(m)
        ]
        units.append(w)

    for w in units:
        w.load_far.start()
        w.load_own.start()
    for w in units:
        for c in w.load_state:
            c.start()

    barrier = pltpu.get_barrier_semaphore()
    peers = [(other_core, z)] + [(partner(i), z) for i in range(m)]
    peers += [(d, (z + k) % n_ex) for k in range(1, n_ex)]
    for peer in peers:
        pl.semaphore_signal(barrier, inc=1, device_id=peer, device_id_type=MESH)
    pl.semaphore_wait(barrier, len(peers))

    def index_in(values, h, s):
        total = 0
        for k, b in enumerate(orders[h][s + 1 :]):
            total = total + values[b] * 2**k
        return total

    def block_sum(w, values, h, s, r):
        q = chip_of(values)
        lanes = slice(h * w.half, (h + 1) * w.half)
        total = w.own[q, r, lanes] + w.s0r[q, r, lanes].astype(F32)
        for past in range(s):
            total = total + w.rcv[past][h, index_in(values, h, past), r, :].astype(F32)
        return total

    def first(w):
        w.load_far.wait()
        step = math.gcd(w.rows, 16384 // w.cols)
        per = w.rows // step

        def body(i):
            q = i // per
            r = pl.ds(pl.multiple_of((i % per) * step, step), step)
            w.s0s[q, r, :] = w.far[q, r, :].astype(BF16)

        loop(chips * per, body)
        w.s0.start()

    def reduce(w, s):
        if s == 0:
            w.load_own.wait()
            w.s0.wait_recv()
        step = math.gcd(w.rows, 16384 // w.half)
        for h in range(2):
            if s > 0:
                w.rs[s - 1][h].wait_recv()
            left = orders[h][s + 1 :]
            for slot in range(2 ** len(left)):
                values = list(bits)
                values[orders[h][s]] = 1 - bits[orders[h][s]]
                for k, b in enumerate(left):
                    values[b] = (slot >> k) & 1

                def body(i):
                    r = pl.ds(pl.multiple_of(i * step, step), step)
                    w.snd[s][h, slot, r, :] = block_sum(w, values, h, s, r).astype(BF16)

                loop(w.rows // step, body)
            w.rs[s][h].start()

    def update(w):
        for c in w.load_state:
            c.wait()
        step = math.gcd(w.rows, 8192 // w.half)
        for h in range(2):
            w.rs[m - 1][h].wait_recv()

            def body(i):
                r = pl.ds(pl.multiple_of(i * step, step), step)
                lanes = slice(h * w.half, (h + 1) * w.half)
                grad = block_sum(w, bits, h, m, r)
                new = adam_update(*(ref[r, lanes] for ref in w.state), grad)
                for ref, value in zip(w.state, new):
                    ref[r, lanes] = value
                block = (d * w.rows + i * step) // BLOCK
                for j in range(w.half // BLOCK):
                    at = h * (w.half // BLOCK) + j
                    if w.u == 0:
                        scale = k_scale[block, at]
                    else:
                        scale = e_scale[z, block, w.dest * (cw // BLOCK) + at]
                    part = new[0][:, j * BLOCK : (j + 1) * BLOCK] / scale
                    part = jnp.clip(part, -LIMIT, LIMIT)
                    cols = slice(at * BLOCK, (at + 1) * BLOCK)
                    if w.u == 0:
                        k_gath[chip, core, r, cols] = part.astype(BF16)
                    else:
                        e_grid[w.u - 1, r, cols] = part.astype(BF16)

            loop(w.rows // step, body)
        for c in w.store_state:
            c.start()
        if w.u == 0:
            gather_send(0)
        else:
            a2a(w.u - 1).start()

    def a2a(t):
        if t == n_ex - 1:
            return pltpu.make_async_copy(e_grid.at[t], o_arr.at[z], a2a_sem.at[t, 0])
        return pltpu.make_async_remote_copy(
            src_ref=e_grid.at[t],
            dst_ref=o_arr.at[z],
            send_sem=a2a_sem.at[t, 0],
            recv_sem=a2a_sem.at[t, 1],
            device_id=(d, place(t)),
            device_id_type=MESH,
        )

    khalf = kwidth // 2

    def gather_copies(s):
        copies = []
        for h in range(2):
            done = orders[h][:s]
            for slot in range(2**s):
                values = list(bits)
                for k, b in enumerate(done):
                    values[b] = (slot >> k) & 1
                ref = k_gath.at[chip_of(values), core, :, pl.ds(h * khalf, khalf)]
                copies.append(
                    pltpu.make_async_remote_copy(
                        src_ref=ref,
                        dst_ref=ref,
                        send_sem=ag_sem.at[s, h, slot, 0],
                        recv_sem=ag_sem.at[s, h, slot, 1],
                        device_id=(partner(orders[h][s]), z),
                        device_id_type=MESH,
                    )
                )
        return copies

    pair = pltpu.make_async_remote_copy(
        src_ref=k_gath.at[:, core],
        dst_ref=k_gath.at[:, core],
        send_sem=pair_sem.at[0],
        recv_sem=pair_sem.at[1],
        device_id=(other_core, z),
        device_id_type=MESH,
    )
    store_key = pltpu.make_async_copy(k_out, o_key, key_sem.at[0])

    def gather_send(s):
        for c in gather_copies(s):
            c.start()

    def gather_next(s):
        for c in gather_copies(s):
            c.wait_recv()
        if s + 1 < m:
            gather_send(s + 1)
        else:
            pair.start()

    def key_finish():
        pair.wait_recv()
        source = lax.broadcasted_iota(jnp.int32, (HD, HD), 0)
        pick = jnp.where(source == order[...], 1.0, 0.0).astype(BF16)
        span = HD // (2 * krows)
        wide = 256
        for head in range(k_out.shape[1] // HD):
            for j in range(kwidth // wide):
                cols = slice(j * wide, (j + 1) * wide)
                block = k_gath[head * span : (head + 1) * span, :, :, cols].reshape(HD, wide)
                turned = lax.dot_general(
                    block, pick, (((0,), (0,)), ((), ())), preferred_element_type=F32
                )
                k_out[cols, head * HD : (head + 1) * HD] = turned.astype(BF16)
        store_key.start()

    stages = [first] + [functools.partial(reduce, s=s) for s in range(m)] + [update]
    extra = [functools.partial(gather_next, s) for s in range(m)] + [key_finish]
    for slot in range(len(units) + len(stages) - 1):
        for s, stage in enumerate(stages):
            if 0 <= slot - s < len(units):
                stage(units[slot - s])
        if 0 <= slot - len(stages) < len(extra):
            extra[slot - len(stages)]()
    for task in extra[len(units) - 1 :]:
        task()

    for t in range(n_ex):
        if t == n_ex - 1:
            a2a(t).wait()
        else:
            a2a(t).wait_send()
            a2a(t).wait_recv()
    for w in units:
        w.s0.wait_send()
        for s in range(m):
            for h in range(2):
                w.rs[s][h].wait_send()
        for c in w.store_state:
            c.wait()
    for s in range(m):
        for c in gather_copies(s):
            c.wait_send()
    pair.wait_send()
    store_key.wait()


def place_slots(n_ex, slot, arrived, placed, sems):
    copies = [
        pltpu.make_async_copy(arrived.at[e], placed.at[slot[e]], sems.at[e]) for e in range(n_ex)
    ]
    for c in copies:
        c.start()
    for c in copies:
        c.wait()


def solution(mesh):
    n_dp, n_ex = mesh.shape["dp"], mesh.shape["expert"]

    def on_device(
        expert_partials,
        key_partials,
        expert_param,
        expert_moment,
        expert_second,
        key_param,
        key_moment,
        key_second,
        expert_scales,
        key_scales,
        rotary_order,
        expert_slot,
    ):
        chips = n_dp // 2
        m = chips.bit_length() - 1
        _, rows, width = expert_param.shape
        krows, kwidth = key_param.shape
        key_rows = key_partials.shape[1]
        cw = width // n_ex
        eg = expert_partials.reshape(chips, 2, rows, width)
        kg = key_partials.reshape(chips, 2, krows, kwidth)
        shape = jax.ShapeDtypeStruct
        anywhere = pl.BlockSpec(memory_space=pl.ANY)
        scalars = pl.BlockSpec(memory_space=pltpu.SMEM)
        vector = pl.BlockSpec(memory_space=pltpu.VMEM)
        dma = pltpu.SemaphoreType.DMA
        counts = [2 ** (m - 1 - s) for s in range(m)]
        out = pl.pallas_call(
            functools.partial(kernel, n_dp, n_ex),
            out_shape=[shape(expert_param.shape, F32)] * 3
            + [shape(key_param.shape, F32)] * 3
            + [shape((n_ex, rows, cw), BF16), shape((kwidth, key_rows), BF16)],
            in_specs=[anywhere] * 8 + [scalars] * 2 + [vector],
            out_specs=[anywhere] * 8,
            scratch_shapes=[
                pltpu.VMEM((n_ex, chips, rows, cw), F32),
                pltpu.VMEM((n_ex, chips, rows, cw), F32),
                pltpu.VMEM((n_ex, chips, rows, cw), BF16),
                pltpu.VMEM((n_ex, chips, rows, cw), BF16),
                pltpu.VMEM((n_ex, 3, rows, cw), F32),
                pltpu.VMEM((n_ex, rows, cw), BF16),
                pltpu.VMEM((chips, krows, kwidth), F32),
                pltpu.VMEM((chips, krows, kwidth), F32),
                pltpu.VMEM((chips, krows, kwidth), BF16),
                pltpu.VMEM((chips, krows, kwidth), BF16),
                pltpu.VMEM((3, krows, kwidth), F32),
                pltpu.VMEM((chips, 2, krows, kwidth), BF16),
                pltpu.VMEM((kwidth, key_rows), BF16),
            ]
            + [pltpu.VMEM((n_ex, 2, c, rows, cw // 2), BF16) for c in counts] * 2
            + [pltpu.VMEM((2, c, krows, kwidth // 2), BF16) for c in counts] * 2
            + [
                dma((n_ex + 1, 5)),
                dma((n_ex + 1, 2)),
                dma((n_ex + 1, m, 2, 2)),
                dma((n_ex + 1, 3)),
                dma((n_ex, 2)),
                dma((m, 2, 2 ** (m - 1), 2)),
                dma((2,)),
                dma((1,)),
            ],
            compiler_params=pltpu.CompilerParams(
                collective_id=0, has_side_effects=True, vmem_limit_bytes=58 * 2**20
            ),
            name="reduce_update_exchange",
        )(
            eg,
            kg,
            expert_param,
            expert_moment,
            expert_second,
            key_param,
            key_moment,
            key_second,
            expert_scales,
            key_scales,
            rotary_order.reshape(1, HD),
        )
        new_ep, new_em, new_es, new_kp, new_km, new_ks, arrived, server_key = out
        placed = pl.pallas_call(
            functools.partial(place_slots, n_ex),
            out_shape=shape(arrived.shape, BF16),
            in_specs=[scalars, anywhere],
            out_specs=anywhere,
            scratch_shapes=[dma((n_ex,))],
            name="place_slots",
        )(expert_slot, arrived)
        server_expert = jnp.transpose(placed, (0, 2, 1))
        return (new_ep, new_em, new_es, new_kp, new_km, new_ks, server_expert, server_key)

    return jax.shard_map(
        on_device,
        mesh=mesh,
        in_specs=(
            P("dp", "expert", None, None),
            P("dp", None, "expert"),
            P("expert", "dp", None),
            P("expert", "dp", None),
            P("expert", "dp", None),
            P("dp", "expert"),
            P("dp", "expert"),
            P("dp", "expert"),
            P(),
            P(None, "expert"),
            P(),
            P(),
        ),
        out_specs=(
            P("expert", "dp", None),
            P("expert", "dp", None),
            P("expert", "dp", None),
            P("dp", "expert"),
            P("dp", "expert"),
            P("dp", "expert"),
            P(None, "expert", "dp"),
            P("expert", None),
        ),
        check_vma=False,
    )
```

```python
import functools
import math

import jax
import jax.numpy as jnp
from jax import lax
from jax.experimental import pallas as pl
from jax.experimental.pallas import tpu as pltpu
from jax.sharding import PartitionSpec as P

HD = 128
BLOCK = 128
BETA_ONE = 0.9
BETA_TWO = 0.95
LEARN = 0.01
DECAY = 0.1
EPSILON = 1e-08
LIMIT = 448.0
CORRECT_ONE = 1.0 - 0.9**10
CORRECT_TWO = 1.0 - 0.95**10
MESH = pl.DeviceIdType.MESH
F32 = jnp.float32
BF16 = jnp.bfloat16


def adam_update(param, moment, second, grad):
    moment = BETA_ONE * moment + (1.0 - BETA_ONE) * grad
    second = BETA_TWO * second + (1.0 - BETA_TWO) * grad * grad
    scaled = moment * (1.0 / CORRECT_ONE)
    corrected = scaled / (jnp.sqrt(second * (1.0 / CORRECT_TWO)) + EPSILON)
    return (param * (1.0 - LEARN * DECAY) - LEARN * corrected, moment, second)


def loop(count, body):
    def step(i, carry):
        body(i)
        return carry

    lax.fori_loop(0, count, step, 0)


def parts_of(cw):
    return max(1, cw // 512 * 2)


def kernel(
    n_dp,
    n_ex,
    eg_hbm,
    kg_hbm,
    ep_hbm,
    em_hbm,
    es_hbm,
    kp_hbm,
    km_hbm,
    ks_hbm,
    e_scale_hbm,
    k_scale_hbm,
    order_hbm,
    o_ep,
    o_em,
    o_es,
    o_kp,
    o_km,
    o_ks,
    o_arr,
    o_key,
    e_far,
    e_own,
    e_s0s,
    e_s0r,
    e_grid,
    k_far,
    k_own,
    k_s0s,
    k_s0r,
    k_gath,
    e_scale,
    k_scale,
    order,
    *rest,
):
    chips = n_dp // 2
    m = chips.bit_length() - 1
    rest = list(rest)
    e_snd = [rest.pop(0) for _ in range(m)]
    e_rcv = [rest.pop(0) for _ in range(m)]
    k_snd = [rest.pop(0) for _ in range(m)]
    k_rcv = [rest.pop(0) for _ in range(m)]
    load_sem, s0_sem, rs_sem, a2a_sem, ag_sem, pair_sem, small_sem = rest

    d = lax.axis_index("dp")
    z = lax.axis_index("expert")
    core = d % 2
    chip = d // 2
    bits = [(chip // 2**i) % 2 for i in range(m)]

    def chip_of(values):
        total = values[0] * 1
        for i in range(1, m):
            total = total + values[i] * 2**i
        return total

    def partner(i):
        return d + (1 - 2 * bits[i]) * 2 ** (i + 1)

    other_core = d + 1 - 2 * core
    orders = (list(range(m)), list(range(m))[::-1])

    rows, width = ep_hbm.shape[1:]
    krows, kwidth = kp_hbm.shape
    cw = width // n_ex
    parts = parts_of(cw)
    uw = cw // parts
    n_units = n_ex * parts

    def place(t):
        return (z + n_ex - 1 - t // parts) % n_ex

    class Unit:
        pass

    units = []
    for u in range(n_units + 1):
        w = Unit()
        w.u = u
        if u == 0:
            w.rows, w.cols = krows, kwidth
            w.columns = pl.ds(0, kwidth)
            w.far, w.own, w.s0s, w.s0r = k_far, k_own, k_s0s, k_s0r
            w.snd, w.rcv = k_snd, k_rcv
            w.grad = kg_hbm
            w.state = [o_kp, o_km, o_ks]
            w.state_in = [kp_hbm, km_hbm, ks_hbm]
        else:
            t = u - 1
            w.dest = place(t)
            w.rows, w.cols = rows, uw
            w.at = t % parts * uw
            w.columns = pl.ds(pl.multiple_of(w.dest * cw + w.at, uw), uw)
            w.far, w.own, w.s0s, w.s0r = (r.at[t] for r in (e_far, e_own, e_s0s, e_s0r))
            w.snd = [r.at[t] for r in e_snd]
            w.rcv = [r.at[t] for r in e_rcv]
            w.grad = eg_hbm
            w.state = [r.at[0, :, w.columns] for r in (o_ep, o_em, o_es)]
            w.state_in = [r.at[0, :, w.columns] for r in (ep_hbm, em_hbm, es_hbm)]
        w.half = w.cols // 2
        w.load_far = pltpu.make_async_copy(
            w.grad.at[:, 1 - core, :, w.columns], w.far, load_sem.at[u, 0]
        )
        w.load_own = pltpu.make_async_copy(
            w.grad.at[:, core, :, w.columns], w.own, load_sem.at[u, 1]
        )
        w.load_state = [
            pltpu.make_async_copy(w.state_in[i], w.state[i], load_sem.at[u, 2 + i])
            for i in range(3)
        ]
        w.s0 = pltpu.make_async_remote_copy(
            src_ref=w.s0s,
            dst_ref=w.s0r,
            send_sem=s0_sem.at[u, 0],
            recv_sem=s0_sem.at[u, 1],
            device_id=(other_core, z),
            device_id_type=MESH,
        )
        w.rs = [
            [
                pltpu.make_async_remote_copy(
                    src_ref=w.snd[s].at[h],
                    dst_ref=w.rcv[s].at[h],
                    send_sem=rs_sem.at[u, s, h, 0],
                    recv_sem=rs_sem.at[u, s, h, 1],
                    device_id=(partner(orders[h][s]), z),
                    device_id_type=MESH,
                )
                for h in range(2)
            ]
            for s in range(m)
        ]
        units.append(w)

    small = [
        pltpu.make_async_copy(source, target, small_sem.at[i])
        for i, (source, target) in enumerate(
            ((k_scale_hbm, k_scale), (e_scale_hbm, e_scale), (order_hbm, order))
        )
    ]
    for w in units:
        w.load_far.start()
        w.load_own.start()
        if w.u == 0:
            for c in small:
                c.start()
    for w in units:
        for c in w.load_state:
            c.start()

    barrier = pltpu.get_barrier_semaphore()
    peers = [(other_core, z)] + [(partner(i), z) for i in range(m)]
    peers += [(d, (z + k) % n_ex) for k in range(1, n_ex)]
    for peer in peers:
        pl.semaphore_signal(barrier, inc=1, device_id=peer, device_id_type=MESH)
    pl.semaphore_wait(barrier, len(peers))

    def index_in(values, h, s):
        total = 0
        for k, b in enumerate(orders[h][s + 1 :]):
            total = total + values[b] * 2**k
        return total

    def block_sum(w, values, h, s, r):
        q = chip_of(values)
        lanes = slice(h * w.half, (h + 1) * w.half)
        total = w.own[q, r, lanes] + w.s0r[q, r, lanes].astype(F32)
        for past in range(s):
            total = total + w.rcv[past][h, index_in(values, h, past), r, :].astype(F32)
        return total

    def first(w):
        w.load_far.wait()
        step = math.gcd(w.rows, 16384 // w.cols)
        per = w.rows // step

        def body(i):
            q = i // per
            r = pl.ds(pl.multiple_of((i % per) * step, step), step)
            w.s0s[q, r, :] = w.far[q, r, :].astype(BF16)

        loop(chips * per, body)
        w.s0.start()

    def reduce(w, s):
        if s == 0:
            w.load_own.wait()
            w.s0.wait_recv()
        step = math.gcd(w.rows, 16384 // w.half)
        for h in range(2):
            if s > 0:
                w.rs[s - 1][h].wait_recv()
            left = orders[h][s + 1 :]
            for slot in range(2 ** len(left)):
                values = list(bits)
                values[orders[h][s]] = 1 - bits[orders[h][s]]
                for k, b in enumerate(left):
                    values[b] = (slot >> k) & 1

                def body(i):
                    r = pl.ds(pl.multiple_of(i * step, step), step)
                    w.snd[s][h, slot, r, :] = block_sum(w, values, h, s, r).astype(BF16)

                loop(w.rows // step, body)
            w.rs[s][h].start()

    def update(w):
        for c in w.load_state:
            c.wait()
        if w.u == 0:
            for c in small:
                c.wait()
        step = math.gcd(w.rows, 8192 // w.half)
        for h in range(2):
            w.rs[m - 1][h].wait_recv()

            def body(i):
                r = pl.ds(pl.multiple_of(i * step, step), step)
                lanes = slice(h * w.half, (h + 1) * w.half)
                grad = block_sum(w, bits, h, m, r)
                new = adam_update(*(ref[r, lanes] for ref in w.state), grad)
                for ref, value in zip(w.state, new):
                    ref[r, lanes] = value
                block = (d * w.rows + i * step) // BLOCK
                for j in range(w.half // BLOCK):
                    at = h * (w.half // BLOCK) + j
                    if w.u == 0:
                        scale = k_scale[block, at]
                    else:
                        scale = e_scale[block, z, w.dest * (cw // BLOCK) + w.at // BLOCK + at]
                    part = new[0][:, j * BLOCK : (j + 1) * BLOCK] / scale
                    part = jnp.clip(part, -LIMIT, LIMIT)
                    cols = slice(at * BLOCK, (at + 1) * BLOCK)
                    if w.u == 0:
                        k_gath[chip, core, r, cols] = part.astype(BF16)
                    elif w.u <= n_units - parts:
                        e_grid[w.u - 1, r, cols] = part.astype(BF16)
                    else:
                        lane = w.at + at * BLOCK
                        o_arr[z, r, lane : lane + BLOCK] = part.astype(BF16)

            loop(w.rows // step, body)
        if w.u == 0:
            gather_send(0)
        elif w.u <= n_units - parts:
            a2a(w.u - 1).start()

    def a2a(t):
        return pltpu.make_async_remote_copy(
            src_ref=e_grid.at[t],
            dst_ref=o_arr.at[z, :, pl.ds(t % parts * uw, uw)],
            send_sem=a2a_sem.at[t, 0],
            recv_sem=a2a_sem.at[t, 1],
            device_id=(d, place(t)),
            device_id_type=MESH,
        )

    khalf = kwidth // 2

    def gather_copies(s):
        copies = []
        for h in range(2):
            done = orders[h][:s]
            for slot in range(2**s):
                values = list(bits)
                for k, b in enumerate(done):
                    values[b] = (slot >> k) & 1
                ref = k_gath.at[chip_of(values), core, :, pl.ds(h * khalf, khalf)]
                copies.append(
                    pltpu.make_async_remote_copy(
                        src_ref=ref,
                        dst_ref=ref,
                        send_sem=ag_sem.at[s, h, slot, 0],
                        recv_sem=ag_sem.at[s, h, slot, 1],
                        device_id=(partner(orders[h][s]), z),
                        device_id_type=MESH,
                    )
                )
        return copies

    pair = pltpu.make_async_remote_copy(
        src_ref=k_gath.at[:, core],
        dst_ref=k_gath.at[:, core],
        send_sem=pair_sem.at[0],
        recv_sem=pair_sem.at[1],
        device_id=(other_core, z),
        device_id_type=MESH,
    )

    def gather_send(s):
        for c in gather_copies(s):
            c.start()

    def gather_next(s):
        for c in gather_copies(s):
            c.wait_recv()
        if s + 1 < m:
            gather_send(s + 1)
        else:
            pair.start()

    def key_finish():
        pair.wait_recv()
        source = lax.broadcasted_iota(jnp.int32, (HD, HD), 0)
        pick = jnp.where(source == order[...], 1.0, 0.0).astype(BF16)
        span = HD // (2 * krows)
        wide = 256
        for head in range(o_key.shape[1] // HD):
            for j in range(kwidth // wide):
                cols = slice(j * wide, (j + 1) * wide)
                block = k_gath[head * span : (head + 1) * span, :, :, cols].reshape(HD, wide)
                turned = lax.dot_general(
                    block, pick, (((0,), (0,)), ((), ())), preferred_element_type=F32
                )
                o_key[cols, head * HD : (head + 1) * HD] = turned.astype(BF16)

    stages = [first] + [functools.partial(reduce, s=s) for s in range(m)] + [update]
    extra = [functools.partial(gather_next, s) for s in range(m)] + [key_finish]
    lags = [0, 1] + [1 + 2 * s for s in range(1, m + 1)]
    for slot in range(len(units) + lags[-1]):
        for stage, lag in zip(stages, lags):
            if 0 <= slot - lag < len(units):
                stage(units[slot - lag])
        if 0 <= slot - lags[-1] - 1 < len(extra):
            extra[slot - lags[-1] - 1]()

    for t in range(n_units - parts):
        a2a(t).wait_send()
        a2a(t).wait_recv()
    for w in units:
        w.s0.wait_send()
        for s in range(m):
            for h in range(2):
                w.rs[s][h].wait_send()
    for s in range(m):
        for c in gather_copies(s):
            c.wait_send()
    pair.wait_send()


def finish(n_ex, slot, *refs):
    sources, targets, sems = refs[:8], refs[8:16], refs[16]
    copies = []
    for i in (0, 1, 2, 7, 3, 4, 5):
        copies.append(pltpu.make_async_copy(sources[i], targets[i], sems.at[i]))
    for e in range(n_ex):
        copies.append(
            pltpu.make_async_copy(sources[6].at[e], targets[6].at[slot[e]], sems.at[8 + e])
        )
    for c in copies:
        c.start()
    for c in copies:
        c.wait()


def solution(mesh):
    n_dp, n_ex = mesh.shape["dp"], mesh.shape["expert"]

    def on_device(
        expert_partials,
        key_partials,
        expert_param,
        expert_moment,
        expert_second,
        key_param,
        key_moment,
        key_second,
        expert_scales,
        key_scales,
        rotary_order,
        expert_slot,
    ):
        chips = n_dp // 2
        m = chips.bit_length() - 1
        _, rows, width = expert_param.shape
        krows, kwidth = key_param.shape
        key_rows = key_partials.shape[1]
        cw = width // n_ex
        parts = parts_of(cw)
        n_units, uw = n_ex * parts, cw // parts
        eg = expert_partials.reshape(chips, 2, rows, width)
        kg = key_partials.reshape(chips, 2, krows, kwidth)
        shape = jax.ShapeDtypeStruct
        anywhere = pl.BlockSpec(memory_space=pl.ANY)
        hbm = pl.BlockSpec(memory_space=pltpu.HBM)
        scalars = pl.BlockSpec(memory_space=pltpu.SMEM)
        vector = pl.BlockSpec(memory_space=pltpu.VMEM)
        dma = pltpu.SemaphoreType.DMA
        counts = [2 ** (m - 1 - s) for s in range(m)]
        out = pl.pallas_call(
            functools.partial(kernel, n_dp, n_ex),
            out_shape=[shape(expert_param.shape, F32)] * 3
            + [shape(key_param.shape, F32)] * 3
            + [shape((n_ex, rows, cw), BF16), shape((kwidth, key_rows), BF16)],
            in_specs=[hbm] * 11,
            out_specs=[vector] * 8,
            scratch_shapes=[
                pltpu.VMEM((n_units, chips, rows, uw), F32),
                pltpu.VMEM((n_units, chips, rows, uw), F32),
                pltpu.VMEM((n_units, chips, rows, uw), BF16),
                pltpu.VMEM((n_units, chips, rows, uw), BF16),
                pltpu.VMEM((n_units - parts, rows, uw), BF16),
                pltpu.VMEM((chips, krows, kwidth), F32),
                pltpu.VMEM((chips, krows, kwidth), F32),
                pltpu.VMEM((chips, krows, kwidth), BF16),
                pltpu.VMEM((chips, krows, kwidth), BF16),
                pltpu.VMEM((chips, 2, krows, kwidth), BF16),
                pltpu.SMEM(expert_scales.shape[1:2] + (n_ex,) + expert_scales.shape[2:], F32),
                pltpu.SMEM(key_scales.shape, F32),
                pltpu.VMEM((1, HD), jnp.int32),
            ]
            + [pltpu.VMEM((n_units, 2, c, rows, uw // 2), BF16) for c in counts] * 2
            + [pltpu.VMEM((2, c, krows, kwidth // 2), BF16) for c in counts] * 2
            + [
                dma((n_units + 1, 5)),
                dma((n_units + 1, 2)),
                dma((n_units + 1, m, 2, 2)),
                dma((n_units - parts, 2)),
                dma((m, 2, 2 ** (m - 1), 2)),
                dma((2,)),
                dma((3,)),
            ],
            compiler_params=pltpu.CompilerParams(
                collective_id=0, has_side_effects=True, vmem_limit_bytes=int(46 * 2**20)
            ),
            name="reduce_update_exchange",
        )(
            eg,
            kg,
            expert_param,
            expert_moment,
            expert_second,
            key_param,
            key_moment,
            key_second,
            jnp.transpose(expert_scales, (1, 0, 2)),
            key_scales,
            rotary_order.reshape(1, HD),
        )
        *state, placed, server_key = pl.pallas_call(
            functools.partial(finish, n_ex),
            out_shape=[shape(x.shape, x.dtype) for x in out],
            in_specs=[scalars] + [vector] * 8,
            out_specs=[anywhere] * 8,
            scratch_shapes=[dma((8 + n_ex,))],
            compiler_params=pltpu.CompilerParams(vmem_limit_bytes=16 * 2**20),
            name="finish",
        )(expert_slot, *out)
        return (*state, jnp.transpose(placed, (0, 2, 1)), server_key)

    return jax.shard_map(
        on_device,
        mesh=mesh,
        in_specs=(
            P("dp", "expert", None, None),
            P("dp", None, "expert"),
            P("expert", "dp", None),
            P("expert", "dp", None),
            P("expert", "dp", None),
            P("dp", "expert"),
            P("dp", "expert"),
            P("dp", "expert"),
            P(),
            P(None, "expert"),
            P(),
            P(),
        ),
        out_specs=(
            P("expert", "dp", None),
            P("expert", "dp", None),
            P("expert", "dp", None),
            P("dp", "expert"),
            P("dp", "expert"),
            P("dp", "expert"),
            P(None, "expert", "dp"),
            P("expert", None),
        ),
        check_vma=False,
    )
```

```python
import functools
import math

import jax
import jax.numpy as jnp
from jax import lax
from jax.experimental import pallas as pl
from jax.experimental.pallas import tpu as pltpu
from jax.sharding import PartitionSpec as P

HD = 128
BLOCK = 128
BETA_ONE = 0.9
BETA_TWO = 0.95
LEARN = 0.01
DECAY = 0.1
EPSILON = 1e-08
LIMIT = 448.0
CORRECT_ONE = 1.0 - 0.9**10
CORRECT_TWO = 1.0 - 0.95**10
MESH = pl.DeviceIdType.MESH
F32 = jnp.float32
BF16 = jnp.bfloat16


def adam_update(param, moment, second, grad):
    moment = BETA_ONE * moment + (1.0 - BETA_ONE) * grad
    second = BETA_TWO * second + (1.0 - BETA_TWO) * grad * grad
    scaled = moment * (1.0 / CORRECT_ONE)
    corrected = scaled / (jnp.sqrt(second * (1.0 / CORRECT_TWO)) + EPSILON)
    return (param * (1.0 - LEARN * DECAY) - LEARN * corrected, moment, second)


def loop(count, body):
    def step(i, carry):
        body(i)
        return carry

    lax.fori_loop(0, count, step, 0)


def parts_of(cw):
    return max(1, cw // 512 * 2)


def kernel(
    n_dp,
    n_ex,
    eg_hbm,
    kg_hbm,
    ep_hbm,
    em_hbm,
    es_hbm,
    kp_hbm,
    km_hbm,
    ks_hbm,
    e_scale_hbm,
    k_scale_hbm,
    order_hbm,
    o_ep,
    o_em,
    o_es,
    o_kp,
    o_km,
    o_ks,
    o_arr,
    o_key,
    e_far,
    e_own,
    e_s0s,
    e_s0r,
    e_grid,
    k_far,
    k_own,
    k_s0s,
    k_s0r,
    k_gath,
    e_scale,
    k_scale,
    order,
    *rest,
):
    chips = n_dp // 2
    m = chips.bit_length() - 1
    rest = list(rest)
    e_snd = [rest.pop(0) for _ in range(m)]
    e_rcv = [rest.pop(0) for _ in range(m)]
    k_snd = [rest.pop(0) for _ in range(m)]
    k_rcv = [rest.pop(0) for _ in range(m)]
    load_sem, s0_sem, rs_sem, a2a_sem, ag_sem, pair_sem, small_sem = rest

    d = lax.axis_index("dp")
    z = lax.axis_index("expert")
    core = d % 2
    chip = d // 2
    bits = [(chip // 2**i) % 2 for i in range(m)]

    def chip_of(values):
        total = values[0] * 1
        for i in range(1, m):
            total = total + values[i] * 2**i
        return total

    def partner(i):
        return d + (1 - 2 * bits[i]) * 2 ** (i + 1)

    other_core = d + 1 - 2 * core
    orders = (list(range(m)), list(range(m))[::-1])

    rows, width = ep_hbm.shape[1:]
    krows, kwidth = kp_hbm.shape
    cw = width // n_ex
    parts = parts_of(cw)
    uw = cw // parts
    n_units = n_ex * parts

    def place(t):
        return (z + n_ex - 1 - t // parts) % n_ex

    class Unit:
        pass

    units = []
    for u in range(n_units + 1):
        w = Unit()
        w.u = u
        if u == 0:
            w.rows, w.cols = krows, kwidth
            w.columns = pl.ds(0, kwidth)
            w.far, w.own, w.s0s, w.s0r = k_far, k_own, k_s0s, k_s0r
            w.snd, w.rcv = k_snd, k_rcv
            w.grad = kg_hbm
            w.state = [o_kp, o_km, o_ks]
            w.state_in = [kp_hbm, km_hbm, ks_hbm]
        else:
            t = u - 1
            w.dest = place(t)
            w.rows, w.cols = rows, uw
            w.at = t % parts * uw
            w.columns = pl.ds(pl.multiple_of(w.dest * cw + w.at, uw), uw)
            w.far, w.own, w.s0s, w.s0r = (r.at[t] for r in (e_far, e_own, e_s0s, e_s0r))
            w.snd = [r.at[t] for r in e_snd]
            w.rcv = [r.at[t] for r in e_rcv]
            w.grad = eg_hbm
            w.state = [r.at[0, :, w.columns] for r in (o_ep, o_em, o_es)]
            w.state_in = [r.at[0, :, w.columns] for r in (ep_hbm, em_hbm, es_hbm)]
        w.half = w.cols // 2
        w.load_far = pltpu.make_async_copy(
            w.grad.at[:, 1 - core, :, w.columns], w.far, load_sem.at[u, 0]
        )
        w.load_own = pltpu.make_async_copy(
            w.grad.at[:, core, :, w.columns], w.own, load_sem.at[u, 1]
        )
        w.load_state = [
            pltpu.make_async_copy(w.state_in[i], w.state[i], load_sem.at[u, 2 + i])
            for i in range(3)
        ]
        w.s0 = pltpu.make_async_remote_copy(
            src_ref=w.s0s,
            dst_ref=w.s0r,
            send_sem=s0_sem.at[u, 0],
            recv_sem=s0_sem.at[u, 1],
            device_id=(other_core, z),
            device_id_type=MESH,
        )
        w.rs = [
            [
                pltpu.make_async_remote_copy(
                    src_ref=w.snd[s].at[h],
                    dst_ref=w.rcv[s].at[h],
                    send_sem=rs_sem.at[u, s, h, 0],
                    recv_sem=rs_sem.at[u, s, h, 1],
                    device_id=(partner(orders[h][s]), z),
                    device_id_type=MESH,
                )
                for h in range(2)
            ]
            for s in range(m)
        ]
        units.append(w)

    small = [
        pltpu.make_async_copy(source, target, small_sem.at[i])
        for i, (source, target) in enumerate(
            ((k_scale_hbm, k_scale), (e_scale_hbm, e_scale), (order_hbm, order))
        )
    ]
    def load(u):
        if 0 <= u < len(units):
            units[u].load_far.start()
            units[u].load_own.start()

    def load_state(u):
        if 0 <= u < len(units):
            for c in units[u].load_state:
                c.start()

    barrier = pltpu.get_barrier_semaphore()
    peers = [(other_core, z)] + [(partner(i), z) for i in range(m)]
    peers += [(d, (z + k) % n_ex) for k in range(1, n_ex)]
    for peer in peers:
        pl.semaphore_signal(barrier, inc=1, device_id=peer, device_id_type=MESH)
    load(0)
    load(1)

    def index_in(values, h, s):
        total = 0
        for k, b in enumerate(orders[h][s + 1 :]):
            total = total + values[b] * 2**k
        return total

    def block_sum(w, values, h, s, r):
        q = chip_of(values)
        lanes = slice(h * w.half, (h + 1) * w.half)
        total = w.own[q, r, lanes] + w.s0r[q, r, lanes].astype(F32)
        for past in range(s):
            total = total + w.rcv[past][h, index_in(values, h, past), r, :].astype(F32)
        return total

    def first(w):
        w.load_far.wait()
        step = math.gcd(w.rows, 16384 // w.cols)
        per = w.rows // step

        def body(i):
            q = i // per
            r = pl.ds(pl.multiple_of((i % per) * step, step), step)
            w.s0s[q, r, :] = w.far[q, r, :].astype(BF16)

        loop(chips * per, body)
        if w.u == 0:
            pl.semaphore_wait(barrier, len(peers))
        w.s0.start()

    def reduce(w, s):
        if s == 0:
            w.load_own.wait()
            w.s0.wait_recv()
        step = math.gcd(w.rows, 16384 // w.half)
        for h in range(2):
            if s > 0:
                w.rs[s - 1][h].wait_recv()
            left = orders[h][s + 1 :]
            for slot in range(2 ** len(left)):
                values = list(bits)
                values[orders[h][s]] = 1 - bits[orders[h][s]]
                for k, b in enumerate(left):
                    values[b] = (slot >> k) & 1

                def body(i):
                    r = pl.ds(pl.multiple_of(i * step, step), step)
                    w.snd[s][h, slot, r, :] = block_sum(w, values, h, s, r).astype(BF16)

                loop(w.rows // step, body)
            w.rs[s][h].start()

    def update(w):
        for c in w.load_state:
            c.wait()
        if w.u == 0:
            for c in small:
                c.wait()
        step = math.gcd(w.rows, 8192 // w.half)
        for h in range(2):
            w.rs[m - 1][h].wait_recv()

            def body(i):
                r = pl.ds(pl.multiple_of(i * step, step), step)
                lanes = slice(h * w.half, (h + 1) * w.half)
                grad = block_sum(w, bits, h, m, r)
                new = adam_update(*(ref[r, lanes] for ref in w.state), grad)
                for ref, value in zip(w.state, new):
                    ref[r, lanes] = value
                block = (d * w.rows + i * step) // BLOCK
                for j in range(w.half // BLOCK):
                    at = h * (w.half // BLOCK) + j
                    if w.u == 0:
                        scale = k_scale[block, at]
                    else:
                        scale = e_scale[block, z, w.dest * (cw // BLOCK) + w.at // BLOCK + at]
                    part = new[0][:, j * BLOCK : (j + 1) * BLOCK] / scale
                    part = jnp.clip(part, -LIMIT, LIMIT)
                    cols = slice(at * BLOCK, (at + 1) * BLOCK)
                    if w.u == 0:
                        k_gath[chip, core, r, cols] = part.astype(BF16)
                    elif w.u <= n_units - parts:
                        e_grid[w.u - 1, r, cols] = part.astype(BF16)
                    else:
                        lane = w.at + at * BLOCK
                        o_arr[z, r, lane : lane + BLOCK] = part.astype(BF16)

            loop(w.rows // step, body)
        if w.u == 0:
            gather_send(0)
        elif w.u <= n_units - parts:
            a2a(w.u - 1).start()
        w.s0.wait_send()
        for s in range(m):
            for h in range(2):
                w.rs[s][h].wait_send()

    def a2a(t):
        return pltpu.make_async_remote_copy(
            src_ref=e_grid.at[t],
            dst_ref=o_arr.at[z, :, pl.ds(t % parts * uw, uw)],
            send_sem=a2a_sem.at[t, 0],
            recv_sem=a2a_sem.at[t, 1],
            device_id=(d, place(t)),
            device_id_type=MESH,
        )

    khalf = kwidth // 2

    def gather_copies(s):
        copies = []
        for h in range(2):
            done = orders[h][:s]
            for slot in range(2**s):
                values = list(bits)
                for k, b in enumerate(done):
                    values[b] = (slot >> k) & 1
                ref = k_gath.at[chip_of(values), core, :, pl.ds(h * khalf, khalf)]
                copies.append(
                    pltpu.make_async_remote_copy(
                        src_ref=ref,
                        dst_ref=ref,
                        send_sem=ag_sem.at[s, h, slot, 0],
                        recv_sem=ag_sem.at[s, h, slot, 1],
                        device_id=(partner(orders[h][s]), z),
                        device_id_type=MESH,
                    )
                )
        return copies

    pair = pltpu.make_async_remote_copy(
        src_ref=k_gath.at[:, core],
        dst_ref=k_gath.at[:, core],
        send_sem=pair_sem.at[0],
        recv_sem=pair_sem.at[1],
        device_id=(other_core, z),
        device_id_type=MESH,
    )

    def gather_send(s):
        for c in gather_copies(s):
            c.start()

    def gather_next(s):
        for c in gather_copies(s):
            c.wait_recv()
        if s + 1 < m:
            gather_send(s + 1)
        else:
            pair.start()

    def key_finish():
        pair.wait_recv()
        source = lax.broadcasted_iota(jnp.int32, (HD, HD), 0)
        pick = jnp.where(source == order[...], 1.0, 0.0).astype(BF16)
        span = HD // (2 * krows)
        wide = 256
        for head in range(o_key.shape[1] // HD):
            for j in range(kwidth // wide):
                cols = slice(j * wide, (j + 1) * wide)
                block = k_gath[head * span : (head + 1) * span, :, :, cols].reshape(HD, wide)
                turned = lax.dot_general(
                    block, pick, (((0,), (0,)), ((), ())), preferred_element_type=F32
                )
                o_key[cols, head * HD : (head + 1) * HD] = turned.astype(BF16)

    stages = [first] + [functools.partial(reduce, s=s) for s in range(m)] + [update]
    lags = [0, 1] + [1 + 2 * s for s in range(1, m)] + [2 * m]
    last = len(units) - 1
    for slot in range(len(units) + lags[-1]):
        for s, (stage, lag) in enumerate(zip(stages, lags)):
            if 0 <= slot - lag <= last:
                stage(units[slot - lag])
            if s == 0:
                load(slot + 2)
                load_state(slot)
                if slot == 0:
                    for c in small:
                        c.start()
            if s == m and slot - lag == last - 1:
                key_finish()
        step = slot - lags[-1] - 1
        if 0 <= step < m:
            gather_next(step)

    for t in range(n_units - parts):
        a2a(t).wait_send()
        a2a(t).wait_recv()
    for s in range(m):
        for c in gather_copies(s):
            c.wait_send()
    pair.wait_send()


def finish(n_ex, slot, *refs):
    sources, targets, sems = refs[:8], refs[8:16], refs[16]
    copies = []
    for i in (0, 1, 2, 7, 3, 4, 5):
        copies.append(pltpu.make_async_copy(sources[i], targets[i], sems.at[i]))
    for e in range(n_ex):
        copies.append(
            pltpu.make_async_copy(sources[6].at[e], targets[6].at[slot[e]], sems.at[8 + e])
        )
    for c in copies:
        c.start()
    for c in copies:
        c.wait()


def solution(mesh):
    n_dp, n_ex = mesh.shape["dp"], mesh.shape["expert"]

    def on_device(
        expert_partials,
        key_partials,
        expert_param,
        expert_moment,
        expert_second,
        key_param,
        key_moment,
        key_second,
        expert_scales,
        key_scales,
        rotary_order,
        expert_slot,
    ):
        chips = n_dp // 2
        m = chips.bit_length() - 1
        _, rows, width = expert_param.shape
        krows, kwidth = key_param.shape
        key_rows = key_partials.shape[1]
        cw = width // n_ex
        parts = parts_of(cw)
        n_units, uw = n_ex * parts, cw // parts
        eg = expert_partials.reshape(chips, 2, rows, width)
        kg = key_partials.reshape(chips, 2, krows, kwidth)
        shape = jax.ShapeDtypeStruct
        anywhere = pl.BlockSpec(memory_space=pl.ANY)
        hbm = pl.BlockSpec(memory_space=pltpu.HBM)
        scalars = pl.BlockSpec(memory_space=pltpu.SMEM)
        vector = pl.BlockSpec(memory_space=pltpu.VMEM)
        dma = pltpu.SemaphoreType.DMA
        counts = [2 ** (m - 1 - s) for s in range(m)]
        here = functools.partial(pltpu.with_memory_space_constraint, memory_space=pltpu.HBM)
        out = pl.pallas_call(
            functools.partial(kernel, n_dp, n_ex),
            out_shape=[shape(expert_param.shape, F32)] * 3
            + [shape(key_param.shape, F32)] * 3
            + [shape((n_ex, rows, cw), BF16), shape((kwidth, key_rows), BF16)],
            in_specs=[hbm] * 11,
            out_specs=[vector] * 8,
            scratch_shapes=[
                pltpu.VMEM((n_units, chips, rows, uw), F32),
                pltpu.VMEM((n_units, chips, rows, uw), F32),
                pltpu.VMEM((n_units, chips, rows, uw), BF16),
                pltpu.VMEM((n_units, chips, rows, uw), BF16),
                pltpu.VMEM((n_units - parts, rows, uw), BF16),
                pltpu.VMEM((chips, krows, kwidth), F32),
                pltpu.VMEM((chips, krows, kwidth), F32),
                pltpu.VMEM((chips, krows, kwidth), BF16),
                pltpu.VMEM((chips, krows, kwidth), BF16),
                pltpu.VMEM((chips, 2, krows, kwidth), BF16),
                pltpu.SMEM(expert_scales.shape[1:2] + (n_ex,) + expert_scales.shape[2:], F32),
                pltpu.SMEM(key_scales.shape, F32),
                pltpu.VMEM((1, HD), jnp.int32),
            ]
            + [pltpu.VMEM((n_units, 2, c, rows, uw // 2), BF16) for c in counts] * 2
            + [pltpu.VMEM((2, c, krows, kwidth // 2), BF16) for c in counts] * 2
            + [
                dma((n_units + 1, 5)),
                dma((n_units + 1, 2)),
                dma((n_units + 1, m, 2, 2)),
                dma((n_units - parts, 2)),
                dma((m, 2, 2 ** (m - 1), 2)),
                dma((2,)),
                dma((3,)),
            ],
            compiler_params=pltpu.CompilerParams(
                collective_id=0, has_side_effects=True, vmem_limit_bytes=int(46 * 2**20)
            ),
            name="reduce_update_exchange",
        )(
            *map(
                here,
                (
                    eg,
                    kg,
                    expert_param,
                    expert_moment,
                    expert_second,
                    key_param,
                    key_moment,
                    key_second,
                    jnp.transpose(expert_scales, (1, 0, 2)),
                    key_scales,
                    rotary_order.reshape(1, HD),
                ),
            )
        )
        *state, placed, server_key = pl.pallas_call(
            functools.partial(finish, n_ex),
            out_shape=[shape(x.shape, x.dtype) for x in out],
            in_specs=[scalars] + [vector] * 8,
            out_specs=[anywhere] * 8,
            scratch_shapes=[dma((8 + n_ex,))],
            compiler_params=pltpu.CompilerParams(vmem_limit_bytes=16 * 2**20),
            name="finish",
        )(expert_slot, *out)
        return (*state, jnp.transpose(placed, (0, 2, 1)), server_key)

    return jax.shard_map(
        on_device,
        mesh=mesh,
        in_specs=(
            P("dp", "expert", None, None),
            P("dp", None, "expert"),
            P("expert", "dp", None),
            P("expert", "dp", None),
            P("expert", "dp", None),
            P("dp", "expert"),
            P("dp", "expert"),
            P("dp", "expert"),
            P(),
            P(None, "expert"),
            P(),
            P(),
        ),
        out_specs=(
            P("expert", "dp", None),
            P("expert", "dp", None),
            P("expert", "dp", None),
            P("dp", "expert"),
            P("dp", "expert"),
            P("dp", "expert"),
            P(None, "expert", "dp"),
            P("expert", None),
        ),
        check_vma=False,
    )
```

```python
import functools
import math

import jax
import jax.numpy as jnp
from jax import lax
from jax.experimental import pallas as pl
from jax.experimental.pallas import tpu as pltpu
from jax.sharding import PartitionSpec as P

HD = 128
BLOCK = 128
BETA_ONE = 0.9
BETA_TWO = 0.95
LEARN = 0.01
DECAY = 0.1
EPSILON = 1e-08
LIMIT = 448.0
CORRECT_ONE = 1.0 - 0.9**10
CORRECT_TWO = 1.0 - 0.95**10
MESH = pl.DeviceIdType.MESH
F32 = jnp.float32
BF16 = jnp.bfloat16


def adam_update(param, moment, second, grad):
    moment = BETA_ONE * moment + (1.0 - BETA_ONE) * grad
    second = BETA_TWO * second + (1.0 - BETA_TWO) * grad * grad
    scaled = moment * (1.0 / CORRECT_ONE)
    corrected = scaled / (jnp.sqrt(second * (1.0 / CORRECT_TWO)) + EPSILON)
    return (param * (1.0 - LEARN * DECAY) - LEARN * corrected, moment, second)


def loop(count, body):
    def step(i, carry):
        body(i)
        return carry

    lax.fori_loop(0, count, step, 0)


def plan(n_ex, cw):
    units = []
    for t in range(n_ex):
        wide = min(cw, 2 * BLOCK)
        sizes = [wide] * (cw // wide)
        if wide > BLOCK and t == 0:
            sizes[:1] = [BLOCK, wide - BLOCK]
        if wide > BLOCK and t == n_ex - 1:
            sizes[-1:] = [wide - BLOCK, BLOCK]
        at = 0
        for size in sizes:
            units.append((t, at, size))
            at += size
    units.insert(2, None)
    return units


def kernel(
    n_dp,
    n_ex,
    eg_hbm,
    kg_hbm,
    ep_hbm,
    em_hbm,
    es_hbm,
    kp_hbm,
    km_hbm,
    ks_hbm,
    e_scale_hbm,
    k_scale_hbm,
    order_hbm,
    o_ep,
    o_em,
    o_es,
    o_kp,
    o_km,
    o_ks,
    o_arr,
    o_key,
    k_gath,
    e_scale,
    k_scale,
    order,
    *rest,
):
    chips = n_dp // 2
    m = chips.bit_length() - 1
    load_sem, s0_sem, rs_sem, a2a_sem, ag_sem, pair_sem, small_sem = rest[:7]
    rest = list(rest[7:])

    d = lax.axis_index("dp")
    z = lax.axis_index("expert")
    core = d % 2
    chip = d // 2
    bits = [(chip // 2**i) % 2 for i in range(m)]

    def chip_of(values):
        total = values[0] * 1
        for i in range(1, m):
            total = total + values[i] * 2**i
        return total

    def partner(i):
        return d + (1 - 2 * bits[i]) * 2 ** (i + 1)

    other_core = d + 1 - 2 * core
    orders = (list(range(m)), list(range(m))[::-1])

    rows, width = ep_hbm.shape[1:]
    krows, kwidth = kp_hbm.shape
    cw = width // n_ex
    layout = plan(n_ex, cw)

    class Unit:
        pass

    units = []
    for u, entry in enumerate(layout):
        w = Unit()
        w.u = u
        w.key = entry is None
        w.far, w.own, w.s0s, w.s0r = (rest.pop(0) for _ in range(4))
        w.snd = [rest.pop(0) for _ in range(m)]
        w.rcv = [rest.pop(0) for _ in range(m)]
        if w.key:
            w.rows, w.cols = krows, kwidth
            w.columns = pl.ds(0, kwidth)
            w.grad = kg_hbm
            w.state = [o_kp, o_km, o_ks]
            w.state_in = [kp_hbm, km_hbm, ks_hbm]
        else:
            t, w.at, w.cols = entry
            w.rows = rows
            w.dest = (z + n_ex - 1 - t) % n_ex
            w.mine = t == n_ex - 1
            w.columns = pl.ds(pl.multiple_of(w.dest * cw + w.at, BLOCK), w.cols)
            w.grad = eg_hbm
            w.state = [r.at[0, :, w.columns] for r in (o_ep, o_em, o_es)]
            w.state_in = [r.at[0, :, w.columns] for r in (ep_hbm, em_hbm, es_hbm)]
            if not w.mine:
                w.grid = rest.pop(0)
                w.exchange = pltpu.make_async_remote_copy(
                    src_ref=w.grid,
                    dst_ref=o_arr.at[z, :, pl.ds(w.at, w.cols)],
                    send_sem=a2a_sem.at[u, 0],
                    recv_sem=a2a_sem.at[u, 1],
                    device_id=(d, w.dest),
                    device_id_type=MESH,
                )
        w.half = w.rows // 2
        w.load_far = pltpu.make_async_copy(
            w.grad.at[:, 1 - core, :, w.columns], w.far, load_sem.at[u, 0]
        )
        w.load_own = pltpu.make_async_copy(
            w.grad.at[:, core, :, w.columns], w.own, load_sem.at[u, 1]
        )
        w.load_state = [
            pltpu.make_async_copy(w.state_in[i], w.state[i], load_sem.at[u, 2 + i])
            for i in range(3)
        ]
        w.s0 = pltpu.make_async_remote_copy(
            src_ref=w.s0s,
            dst_ref=w.s0r,
            send_sem=s0_sem.at[u, 0],
            recv_sem=s0_sem.at[u, 1],
            device_id=(other_core, z),
            device_id_type=MESH,
        )
        w.rs = [
            [
                pltpu.make_async_remote_copy(
                    src_ref=w.snd[s].at[h],
                    dst_ref=w.rcv[s].at[h],
                    send_sem=rs_sem.at[u, s, h, 0],
                    recv_sem=rs_sem.at[u, s, h, 1],
                    device_id=(partner(orders[h][s]), z),
                    device_id_type=MESH,
                )
                for h in range(2)
            ]
            for s in range(m)
        ]
        units.append(w)

    small = [
        pltpu.make_async_copy(source, target, small_sem.at[i])
        for i, (source, target) in enumerate(
            ((k_scale_hbm, k_scale), (e_scale_hbm, e_scale), (order_hbm, order))
        )
    ]
    def load(u):
        if 0 <= u < len(units):
            units[u].load_far.start()
            units[u].load_own.start()

    def load_state(u):
        if 0 <= u < len(units):
            for c in units[u].load_state:
                c.start()

    barrier = pltpu.get_barrier_semaphore()
    peers = [(other_core, z)] + [(partner(i), z) for i in range(m)]
    peers += [(d, (z + k) % n_ex) for k in range(1, n_ex)]
    for peer in peers:
        pl.semaphore_signal(barrier, inc=1, device_id=peer, device_id_type=MESH)
    load(0)
    load(1)

    def index_in(values, h, s):
        total = 0
        for k, b in enumerate(orders[h][s + 1 :]):
            total = total + values[b] * 2**k
        return total

    def rows_at(i, step):
        return pl.ds(pl.multiple_of(i * step, step), step)

    def rows_in(w, h, i, step):
        return pl.ds(pl.multiple_of(h * w.half + i * step, step), step)

    def block_sum(w, values, h, s, i, step):
        q = chip_of(values)
        r, whole = rows_at(i, step), rows_in(w, h, i, step)
        total = w.own[q, whole, :] + w.s0r[q, whole, :].astype(F32)
        for past in range(s):
            total = total + w.rcv[past][h, index_in(values, h, past), r, :].astype(F32)
        return total

    def first(w):
        w.load_far.wait()
        step = math.gcd(w.rows, 16384 // w.cols)
        per = w.rows // step

        def body(i):
            q = i // per
            r = pl.ds(pl.multiple_of((i % per) * step, step), step)
            w.s0s[q, r, :] = w.far[q, r, :].astype(BF16)

        loop(chips * per, body)
        if w.u == 0:
            pl.semaphore_wait(barrier, len(peers))
        w.s0.start()

    def reduce(w, s):
        if s == 0:
            w.load_own.wait()
            w.s0.wait_recv()
        step = math.gcd(w.half, 16384 // w.cols)
        for h in range(2):
            if s > 0:
                w.rs[s - 1][h].wait_recv()
            left = orders[h][s + 1 :]
            for slot in range(2 ** len(left)):
                values = list(bits)
                values[orders[h][s]] = 1 - bits[orders[h][s]]
                for k, b in enumerate(left):
                    values[b] = (slot >> k) & 1

                def body(i):
                    total = block_sum(w, values, h, s, i, step)
                    w.snd[s][h, slot, rows_at(i, step), :] = total.astype(BF16)

                loop(w.half // step, body)
            w.rs[s][h].start()

    def update(w):
        for c in w.load_state:
            c.wait()
        if w.u == 0:
            for c in small:
                c.wait()
        step = math.gcd(w.half, max(16, 8192 // w.cols))
        for h in range(2):
            w.rs[m - 1][h].wait_recv()

            def body(i):
                r = rows_in(w, h, i, step)
                grad = block_sum(w, bits, h, m, i, step)
                new = adam_update(*(ref[r, :] for ref in w.state), grad)
                for ref, value in zip(w.state, new):
                    ref[r, :] = value
                block = (d * w.rows + h * w.half + i * step) // BLOCK
                for j in range(w.cols // BLOCK):
                    if w.key:
                        scale = k_scale[block, j]
                    else:
                        scale = e_scale[block, z, w.dest * (cw // BLOCK) + w.at // BLOCK + j]
                    cols = slice(j * BLOCK, (j + 1) * BLOCK)
                    part = jnp.clip(new[0][:, cols] / scale, -LIMIT, LIMIT).astype(BF16)
                    if w.key:
                        k_gath[chip, core, r, cols] = part
                    elif w.mine:
                        o_arr[z, r, w.at + j * BLOCK : w.at + (j + 1) * BLOCK] = part
                    else:
                        w.grid[r, cols] = part

            loop(w.half // step, body)
        if w.key:
            gather_send(0)
        elif not w.mine:
            w.exchange.start()
        w.s0.wait_send()
        for s in range(m):
            for h in range(2):
                w.rs[s][h].wait_send()

    khalf = kwidth // 2

    def gather_copies(s):
        copies = []
        for h in range(2):
            done = orders[h][:s]
            for slot in range(2**s):
                values = list(bits)
                for k, b in enumerate(done):
                    values[b] = (slot >> k) & 1
                ref = k_gath.at[chip_of(values), core, :, pl.ds(h * khalf, khalf)]
                copies.append(
                    pltpu.make_async_remote_copy(
                        src_ref=ref,
                        dst_ref=ref,
                        send_sem=ag_sem.at[s, h, slot, 0],
                        recv_sem=ag_sem.at[s, h, slot, 1],
                        device_id=(partner(orders[h][s]), z),
                        device_id_type=MESH,
                    )
                )
        return copies

    pair = pltpu.make_async_remote_copy(
        src_ref=k_gath.at[:, core],
        dst_ref=k_gath.at[:, core],
        send_sem=pair_sem.at[0],
        recv_sem=pair_sem.at[1],
        device_id=(other_core, z),
        device_id_type=MESH,
    )

    def gather_send(s):
        for c in gather_copies(s):
            c.start()

    def gather_next(s):
        for c in gather_copies(s):
            c.wait_recv()
        if s + 1 < m:
            gather_send(s + 1)
        else:
            pair.start()

    def key_finish():
        pair.wait_recv()
        source = lax.broadcasted_iota(jnp.int32, (HD, HD), 0)
        pick = jnp.where(source == order[...], 1.0, 0.0).astype(BF16)
        span = HD // (2 * krows)
        wide = 256
        for head in range(o_key.shape[1] // HD):
            for j in range(kwidth // wide):
                cols = slice(j * wide, (j + 1) * wide)
                block = k_gath[head * span : (head + 1) * span, :, :, cols].reshape(HD, wide)
                turned = lax.dot_general(
                    block, pick, (((0,), (0,)), ((), ())), preferred_element_type=F32
                )
                o_key[cols, head * HD : (head + 1) * HD] = turned.astype(BF16)

    stages = [first] + [functools.partial(reduce, s=s) for s in range(m)] + [update]
    lags = [0, 1] + [1 + 2 * s for s in range(1, m)] + [2 * m]
    last = len(units) - 1
    for slot in range(len(units) + lags[-1]):
        for s, (stage, lag) in enumerate(zip(stages, lags)):
            if 0 <= slot - lag <= last:
                stage(units[slot - lag])
            if s == 0:
                load(slot + 2)
                load_state(slot)
                if slot == 0:
                    for c in small:
                        c.start()
            if s == m and slot - lag == last - 1:
                key_finish()
        step = slot - lags[-1] - 1 - layout.index(None)
        if 0 <= step < m:
            gather_next(step)

    for w in units:
        if not w.key and not w.mine:
            w.exchange.wait_send()
            w.exchange.wait_recv()
    for s in range(m):
        for c in gather_copies(s):
            c.wait_send()
    pair.wait_send()


def finish(n_ex, slot, *refs):
    sources, targets, sems = refs[:8], refs[8:16], refs[16]
    pairs = []
    for i in range(3):
        part = sources[i].shape[1] // 4
        for k in range(4):
            at = pl.ds(k * part, part)
            pairs.append((sources[i].at[:, at], targets[i].at[:, at]))
    for i in (7, 3, 4, 5):
        pairs.append((sources[i], targets[i]))
    for e in range(n_ex):
        pairs.append((sources[6].at[e], targets[6].at[slot[e]]))
    copies = [pltpu.make_async_copy(a, b, sems.at[i]) for i, (a, b) in enumerate(pairs)]
    for c in copies:
        c.start()
    for c in copies:
        c.wait()


def solution(mesh):
    n_dp, n_ex = mesh.shape["dp"], mesh.shape["expert"]

    def on_device(
        expert_partials,
        key_partials,
        expert_param,
        expert_moment,
        expert_second,
        key_param,
        key_moment,
        key_second,
        expert_scales,
        key_scales,
        rotary_order,
        expert_slot,
    ):
        chips = n_dp // 2
        m = chips.bit_length() - 1
        _, rows, width = expert_param.shape
        krows, kwidth = key_param.shape
        key_rows = key_partials.shape[1]
        cw = width // n_ex
        layout = plan(n_ex, cw)
        eg = expert_partials.reshape(chips, 2, rows, width)
        kg = key_partials.reshape(chips, 2, krows, kwidth)
        shape = jax.ShapeDtypeStruct
        anywhere = pl.BlockSpec(memory_space=pl.ANY)
        hbm = pl.BlockSpec(memory_space=pltpu.HBM)
        scalars = pl.BlockSpec(memory_space=pltpu.SMEM)
        vector = pl.BlockSpec(memory_space=pltpu.VMEM)
        dma = pltpu.SemaphoreType.DMA
        buffers = []
        for entry in layout:
            high, wide = (krows, kwidth) if entry is None else (rows, entry[2])
            buffers += [pltpu.VMEM((chips, high, wide), t) for t in (F32, F32, BF16, BF16)]
            steps = [
                pltpu.VMEM((2, 2 ** (m - 1 - s), high // 2, wide), BF16) for s in range(m)
            ]
            buffers += steps + steps
            if entry is not None and entry[0] < n_ex - 1:
                buffers.append(pltpu.VMEM((high, wide), BF16))
        here = functools.partial(pltpu.with_memory_space_constraint, memory_space=pltpu.HBM)
        out = pl.pallas_call(
            functools.partial(kernel, n_dp, n_ex),
            out_shape=[shape(expert_param.shape, F32)] * 3
            + [shape(key_param.shape, F32)] * 3
            + [shape((n_ex, rows, cw), BF16), shape((kwidth, key_rows), BF16)],
            in_specs=[hbm] * 11,
            out_specs=[vector] * 8,
            scratch_shapes=[
                pltpu.VMEM((chips, 2, krows, kwidth), BF16),
                pltpu.SMEM(expert_scales.shape[1:2] + (n_ex,) + expert_scales.shape[2:], F32),
                pltpu.SMEM(key_scales.shape, F32),
                pltpu.VMEM((1, HD), jnp.int32),
                dma((len(layout), 5)),
                dma((len(layout), 2)),
                dma((len(layout), m, 2, 2)),
                dma((len(layout), 2)),
                dma((m, 2, 2 ** (m - 1), 2)),
                dma((2,)),
                dma((3,)),
            ]
            + buffers,
            compiler_params=pltpu.CompilerParams(
                collective_id=0, has_side_effects=True, vmem_limit_bytes=int(46 * 2**20)
            ),
            name="reduce_update_exchange",
        )(
            *map(
                here,
                (
                    eg,
                    kg,
                    expert_param,
                    expert_moment,
                    expert_second,
                    key_param,
                    key_moment,
                    key_second,
                    jnp.transpose(expert_scales, (1, 0, 2)),
                    key_scales,
                    rotary_order.reshape(1, HD),
                ),
            )
        )
        *state, placed, server_key = pl.pallas_call(
            functools.partial(finish, n_ex),
            out_shape=[shape(x.shape, x.dtype) for x in out],
            in_specs=[scalars] + [vector] * 8,
            out_specs=[anywhere] * 8,
            scratch_shapes=[dma((16 + n_ex,))],
            compiler_params=pltpu.CompilerParams(vmem_limit_bytes=16 * 2**20),
            name="finish",
        )(expert_slot, *out)
        return (*state, jnp.transpose(placed, (0, 2, 1)), server_key)

    return jax.shard_map(
        on_device,
        mesh=mesh,
        in_specs=(
            P("dp", "expert", None, None),
            P("dp", None, "expert"),
            P("expert", "dp", None),
            P("expert", "dp", None),
            P("expert", "dp", None),
            P("dp", "expert"),
            P("dp", "expert"),
            P("dp", "expert"),
            P(),
            P(None, "expert"),
            P(),
            P(),
        ),
        out_specs=(
            P("expert", "dp", None),
            P("expert", "dp", None),
            P("expert", "dp", None),
            P("dp", "expert"),
            P("dp", "expert"),
            P("dp", "expert"),
            P(None, "expert", "dp"),
            P("expert", None),
        ),
        check_vma=False,
    )
```

```python
import functools
import math

import jax
import jax.numpy as jnp
from jax import lax
from jax.experimental import pallas as pl
from jax.experimental.pallas import tpu as pltpu
from jax.sharding import PartitionSpec as P

HD = 128
BLOCK = 128
BETA_ONE = 0.9
BETA_TWO = 0.95
LEARN = 0.01
DECAY = 0.1
EPSILON = 1e-08
LIMIT = 448.0
CORRECT_ONE = 1.0 - 0.9**10
CORRECT_TWO = 1.0 - 0.95**10
MESH = pl.DeviceIdType.MESH
F32 = jnp.float32
BF16 = jnp.bfloat16


def adam_update(param, moment, second, grad):
    moment = BETA_ONE * moment + (1.0 - BETA_ONE) * grad
    second = BETA_TWO * second + (1.0 - BETA_TWO) * grad * grad
    scaled = moment * (1.0 / CORRECT_ONE)
    corrected = scaled / (jnp.sqrt(second * (1.0 / CORRECT_TWO)) + EPSILON)
    return (param * (1.0 - LEARN * DECAY) - LEARN * corrected, moment, second)


def loop(count, body):
    def step(i, carry):
        body(i)
        return carry

    lax.fori_loop(0, count, step, 0)


def plan(n_ex, cw):
    units = []
    for t in range(n_ex):
        wide = min(cw, 2 * BLOCK)
        sizes = [wide] * (cw // wide)
        if wide > BLOCK and t == 0:
            sizes[:1] = [BLOCK, wide - BLOCK]
        if wide > BLOCK and t == n_ex - 1:
            sizes[-1:] = [wide - BLOCK, BLOCK]
        at = 0
        for size in sizes:
            units.append((t, at, size))
            at += size
    units.insert(2, None)
    return units


def kernel(
    n_dp,
    n_ex,
    eg_hbm,
    kg_hbm,
    ep_hbm,
    em_hbm,
    es_hbm,
    kp_hbm,
    km_hbm,
    ks_hbm,
    e_scale_hbm,
    k_scale_hbm,
    order_hbm,
    o_ep,
    o_em,
    o_es,
    o_kp,
    o_km,
    o_ks,
    o_arr,
    o_key,
    k_gath,
    e_scale,
    k_scale,
    order,
    *rest,
):
    chips = n_dp // 2
    m = chips.bit_length() - 1
    load_sem, s0_sem, rs_sem, a2a_sem, ag_sem, pair_sem, small_sem, ready = rest[:8]
    rest = list(rest[8:])

    d = lax.axis_index("dp")
    z = lax.axis_index("expert")
    core = d % 2
    chip = d // 2
    bits = [(chip // 2**i) % 2 for i in range(m)]

    def chip_of(values):
        total = values[0] * 1
        for i in range(1, m):
            total = total + values[i] * 2**i
        return total

    def partner(i):
        return d + (1 - 2 * bits[i]) * 2 ** (i + 1)

    other_core = d + 1 - 2 * core
    orders = (list(range(m)), list(range(m))[::-1])

    rows, width = ep_hbm.shape[1:]
    krows, kwidth = kp_hbm.shape
    cw = width // n_ex
    layout = plan(n_ex, cw)

    class Unit:
        pass

    units = []
    for u, entry in enumerate(layout):
        w = Unit()
        w.u = u
        w.key = entry is None
        w.far, w.own, w.s0s, w.s0r = (rest.pop(0) for _ in range(4))
        w.snd = [rest.pop(0) for _ in range(m)]
        w.rcv = [rest.pop(0) for _ in range(m)]
        if w.key:
            w.rows, w.cols = krows, kwidth
            w.columns = pl.ds(0, kwidth)
            w.grad = kg_hbm
            w.state = [o_kp, o_km, o_ks]
            w.state_in = [kp_hbm, km_hbm, ks_hbm]
        else:
            t, w.at, w.cols = entry
            w.rows = rows
            w.dest = (z + n_ex - 1 - t) % n_ex
            w.mine = t == n_ex - 1
            w.columns = pl.ds(pl.multiple_of(w.dest * cw + w.at, BLOCK), w.cols)
            w.grad = eg_hbm
            w.state = [r.at[0, :, w.columns] for r in (o_ep, o_em, o_es)]
            w.state_in = [r.at[0, :, w.columns] for r in (ep_hbm, em_hbm, es_hbm)]
            if not w.mine:
                w.grid = rest.pop(0)
                w.exchange = pltpu.make_async_remote_copy(
                    src_ref=w.grid,
                    dst_ref=o_arr.at[z, :, pl.ds(w.at, w.cols)],
                    send_sem=a2a_sem.at[u, 0],
                    recv_sem=a2a_sem.at[u, 1],
                    device_id=(d, w.dest),
                    device_id_type=MESH,
                )
        w.half = w.rows // 2
        w.load_far = pltpu.make_async_copy(
            w.grad.at[:, 1 - core, :, w.columns], w.far, load_sem.at[u, 0]
        )
        w.load_own = pltpu.make_async_copy(
            w.grad.at[:, core, :, w.columns], w.own, load_sem.at[u, 1]
        )
        w.load_state = [
            pltpu.make_async_copy(w.state_in[i], w.state[i], load_sem.at[u, 2 + i])
            for i in range(3)
        ]
        w.s0 = pltpu.make_async_remote_copy(
            src_ref=w.s0s,
            dst_ref=w.s0r,
            send_sem=s0_sem.at[u, 0],
            recv_sem=s0_sem.at[u, 1],
            device_id=(other_core, z),
            device_id_type=MESH,
        )
        w.rs = [
            [
                pltpu.make_async_remote_copy(
                    src_ref=w.snd[s].at[h],
                    dst_ref=w.rcv[s].at[h],
                    send_sem=rs_sem.at[u, s, h, 0],
                    recv_sem=rs_sem.at[u, s, h, 1],
                    device_id=(partner(orders[h][s]), z),
                    device_id_type=MESH,
                )
                for h in range(2)
            ]
            for s in range(m)
        ]
        units.append(w)

    small = [
        pltpu.make_async_copy(source, target, small_sem.at[i])
        for i, (source, target) in enumerate(
            ((k_scale_hbm, k_scale), (e_scale_hbm, e_scale), (order_hbm, order))
        )
    ]
    def load(u):
        if 0 <= u < len(units):
            units[u].load_far.start()
            units[u].load_own.start()

    def load_state(u):
        if 0 <= u < len(units):
            for c in units[u].load_state:
                c.start()

    barrier = pltpu.get_barrier_semaphore()
    for k in range(1, chips):
        pl.semaphore_signal(
            barrier, inc=1, device_id=((chip + k) % chips * 2, z), device_id_type=MESH
        )

    @pl.when(core == 1)
    def _():
        pl.semaphore_signal(barrier, inc=1, device_id=(other_core, z), device_id_type=MESH)

    def plane_ready():
        @pl.when(core == 0)
        def _():
            pl.semaphore_wait(barrier, 2 * chips - 1)
            pl.semaphore_signal(
                ready.at[0], inc=1, device_id=(other_core, z), device_id_type=MESH
            )

        @pl.when(core == 1)
        def _():
            pl.semaphore_wait(ready.at[0], 1)
            for k in range(1, n_ex):
                pl.semaphore_signal(
                    barrier, inc=1, device_id=(d, (z + k) % n_ex), device_id_type=MESH
                )

    def planes_ready():
        @pl.when(core == 1)
        def _():
            pl.semaphore_wait(barrier, n_ex - 1)
            pl.semaphore_signal(
                ready.at[1], inc=1, device_id=(other_core, z), device_id_type=MESH
            )

        @pl.when(core == 0)
        def _():
            pl.semaphore_wait(ready.at[1], 1)

    load(0)
    load(1)

    def index_in(values, h, s):
        total = 0
        for k, b in enumerate(orders[h][s + 1 :]):
            total = total + values[b] * 2**k
        return total

    def rows_at(i, step):
        return pl.ds(pl.multiple_of(i * step, step), step)

    def rows_in(w, h, i, step):
        return pl.ds(pl.multiple_of(h * w.half + i * step, step), step)

    def block_sum(w, values, h, s, i, step):
        q = chip_of(values)
        r, whole = rows_at(i, step), rows_in(w, h, i, step)
        total = w.own[q, whole, :] + w.s0r[q, whole, :].astype(F32)
        for past in range(s):
            total = total + w.rcv[past][h, index_in(values, h, past), r, :].astype(F32)
        return total

    def first(w):
        w.load_far.wait()
        step = math.gcd(w.rows, 16384 // w.cols)
        per = w.rows // step

        def body(i):
            q = i // per
            r = pl.ds(pl.multiple_of((i % per) * step, step), step)
            w.s0s[q, r, :] = w.far[q, r, :].astype(BF16)

        loop(chips * per, body)
        if w.u == 0:
            plane_ready()
        w.s0.start()

    def reduce(w, s):
        if s == 0:
            w.load_own.wait()
            w.s0.wait_recv()
        step = math.gcd(w.half, 16384 // w.cols)
        for h in range(2):
            if s > 0:
                w.rs[s - 1][h].wait_recv()
            left = orders[h][s + 1 :]
            for slot in range(2 ** len(left)):
                values = list(bits)
                values[orders[h][s]] = 1 - bits[orders[h][s]]
                for k, b in enumerate(left):
                    values[b] = (slot >> k) & 1

                def body(i):
                    total = block_sum(w, values, h, s, i, step)
                    w.snd[s][h, slot, rows_at(i, step), :] = total.astype(BF16)

                loop(w.half // step, body)
            w.rs[s][h].start()

    def update(w):
        for c in w.load_state:
            c.wait()
        if w.u == 0:
            for c in small:
                c.wait()
        step = math.gcd(w.half, max(16, 8192 // w.cols))
        for h in range(2):
            w.rs[m - 1][h].wait_recv()

            def body(i):
                r = rows_in(w, h, i, step)
                grad = block_sum(w, bits, h, m, i, step)
                new = adam_update(*(ref[r, :] for ref in w.state), grad)
                for ref, value in zip(w.state, new):
                    ref[r, :] = value
                block = (d * w.rows + h * w.half + i * step) // BLOCK
                for j in range(w.cols // BLOCK):
                    if w.key:
                        scale = k_scale[block, j]
                    else:
                        scale = e_scale[block, z, w.dest * (cw // BLOCK) + w.at // BLOCK + j]
                    cols = slice(j * BLOCK, (j + 1) * BLOCK)
                    part = jnp.clip(new[0][:, cols] / scale, -LIMIT, LIMIT).astype(BF16)
                    if w.key:
                        k_gath[chip, core, r, cols] = part
                    elif w.mine:
                        o_arr[z, r, w.at + j * BLOCK : w.at + (j + 1) * BLOCK] = part
                    else:
                        w.grid[r, cols] = part

            loop(w.half // step, body)
        if w.key:
            gather_send(0)
        elif not w.mine:
            if w.u == 0:
                planes_ready()
            w.exchange.start()
        w.s0.wait_send()
        for s in range(m):
            for h in range(2):
                w.rs[s][h].wait_send()

    khalf = kwidth // 2

    def gather_copies(s):
        copies = []
        for h in range(2):
            done = orders[h][:s]
            for slot in range(2**s):
                values = list(bits)
                for k, b in enumerate(done):
                    values[b] = (slot >> k) & 1
                ref = k_gath.at[chip_of(values), core, :, pl.ds(h * khalf, khalf)]
                copies.append(
                    pltpu.make_async_remote_copy(
                        src_ref=ref,
                        dst_ref=ref,
                        send_sem=ag_sem.at[s, h, slot, 0],
                        recv_sem=ag_sem.at[s, h, slot, 1],
                        device_id=(partner(orders[h][s]), z),
                        device_id_type=MESH,
                    )
                )
        return copies

    pair = pltpu.make_async_remote_copy(
        src_ref=k_gath.at[:, core],
        dst_ref=k_gath.at[:, core],
        send_sem=pair_sem.at[0],
        recv_sem=pair_sem.at[1],
        device_id=(other_core, z),
        device_id_type=MESH,
    )

    def gather_send(s):
        for c in gather_copies(s):
            c.start()

    def gather_next(s):
        for c in gather_copies(s):
            c.wait_recv()
        if s + 1 < m:
            gather_send(s + 1)
        else:
            pair.start()

    def key_finish():
        pair.wait_recv()
        source = lax.broadcasted_iota(jnp.int32, (HD, HD), 0)
        pick = jnp.where(source == order[...], 1.0, 0.0).astype(BF16)
        span = HD // (2 * krows)
        wide = 256
        for head in range(o_key.shape[1] // HD):
            for j in range(kwidth // wide):
                cols = slice(j * wide, (j + 1) * wide)
                block = k_gath[head * span : (head + 1) * span, :, :, cols].reshape(HD, wide)
                turned = lax.dot_general(
                    block, pick, (((0,), (0,)), ((), ())), preferred_element_type=F32
                )
                o_key[cols, head * HD : (head + 1) * HD] = turned.astype(BF16)

    stages = [first] + [functools.partial(reduce, s=s) for s in range(m)] + [update]
    lags = [0, 1] + [2 + 2 * s for s in range(1, m)] + [2 * m + 1]
    last = len(units) - 1
    for slot in range(len(units) + lags[-1]):
        for s, (stage, lag) in enumerate(zip(stages, lags)):
            if 0 <= slot - lag <= last:
                stage(units[slot - lag])
            if s == 0:
                load(slot + 2)
                load_state(slot)
                if slot == 0:
                    for c in small:
                        c.start()
            if s == m and slot - lag == last - 1:
                key_finish()
        step = slot - lags[-1] - 1 - layout.index(None)
        if 0 <= step < m:
            gather_next(step)

    for w in units:
        if not w.key and not w.mine:
            w.exchange.wait_send()
            w.exchange.wait_recv()
    for s in range(m):
        for c in gather_copies(s):
            c.wait_send()
    pair.wait_send()


def finish(n_ex, slot, *refs):
    sources, targets, sems = refs[:8], refs[8:16], refs[16]
    pairs = []
    for i in range(3):
        part = sources[i].shape[1] // 4
        for k in range(4):
            at = pl.ds(k * part, part)
            pairs.append((sources[i].at[:, at], targets[i].at[:, at]))
    for i in (7, 3, 4, 5):
        pairs.append((sources[i], targets[i]))
    for e in range(n_ex):
        pairs.append((sources[6].at[e], targets[6].at[slot[e]]))
    copies = [pltpu.make_async_copy(a, b, sems.at[i]) for i, (a, b) in enumerate(pairs)]
    for c in copies:
        c.start()
    for c in copies:
        c.wait()


def solution(mesh):
    n_dp, n_ex = mesh.shape["dp"], mesh.shape["expert"]

    def on_device(
        expert_partials,
        key_partials,
        expert_param,
        expert_moment,
        expert_second,
        key_param,
        key_moment,
        key_second,
        expert_scales,
        key_scales,
        rotary_order,
        expert_slot,
    ):
        chips = n_dp // 2
        m = chips.bit_length() - 1
        _, rows, width = expert_param.shape
        krows, kwidth = key_param.shape
        key_rows = key_partials.shape[1]
        cw = width // n_ex
        layout = plan(n_ex, cw)
        eg = expert_partials.reshape(chips, 2, rows, width)
        kg = key_partials.reshape(chips, 2, krows, kwidth)
        shape = jax.ShapeDtypeStruct
        anywhere = pl.BlockSpec(memory_space=pl.ANY)
        hbm = pl.BlockSpec(memory_space=pltpu.HBM)
        scalars = pl.BlockSpec(memory_space=pltpu.SMEM)
        vector = pl.BlockSpec(memory_space=pltpu.VMEM)
        dma = pltpu.SemaphoreType.DMA
        buffers = []
        for entry in layout:
            high, wide = (krows, kwidth) if entry is None else (rows, entry[2])
            buffers += [pltpu.VMEM((chips, high, wide), t) for t in (F32, F32, BF16, BF16)]
            steps = [
                pltpu.VMEM((2, 2 ** (m - 1 - s), high // 2, wide), BF16) for s in range(m)
            ]
            buffers += steps + steps
            if entry is not None and entry[0] < n_ex - 1:
                buffers.append(pltpu.VMEM((high, wide), BF16))
        here = functools.partial(pltpu.with_memory_space_constraint, memory_space=pltpu.HBM)
        out = pl.pallas_call(
            functools.partial(kernel, n_dp, n_ex),
            out_shape=[shape(expert_param.shape, F32)] * 3
            + [shape(key_param.shape, F32)] * 3
            + [shape((n_ex, rows, cw), BF16), shape((kwidth, key_rows), BF16)],
            in_specs=[hbm] * 11,
            out_specs=[vector] * 8,
            scratch_shapes=[
                pltpu.VMEM((chips, 2, krows, kwidth), BF16),
                pltpu.SMEM(expert_scales.shape[1:2] + (n_ex,) + expert_scales.shape[2:], F32),
                pltpu.SMEM(key_scales.shape, F32),
                pltpu.VMEM((1, HD), jnp.int32),
                dma((len(layout), 5)),
                dma((len(layout), 2)),
                dma((len(layout), m, 2, 2)),
                dma((len(layout), 2)),
                dma((m, 2, 2 ** (m - 1), 2)),
                dma((2,)),
                dma((3,)),
                pltpu.SemaphoreType.REGULAR((2,)),
            ]
            + buffers,
            compiler_params=pltpu.CompilerParams(
                collective_id=0, has_side_effects=True, vmem_limit_bytes=int(46 * 2**20)
            ),
            name="reduce_update_exchange",
        )(
            *map(
                here,
                (
                    eg,
                    kg,
                    expert_param,
                    expert_moment,
                    expert_second,
                    key_param,
                    key_moment,
                    key_second,
                    jnp.transpose(expert_scales, (1, 0, 2)),
                    key_scales,
                    rotary_order.reshape(1, HD),
                ),
            )
        )
        *state, placed, server_key = pl.pallas_call(
            functools.partial(finish, n_ex),
            out_shape=[shape(x.shape, x.dtype) for x in out],
            in_specs=[scalars] + [vector] * 8,
            out_specs=[anywhere] * 8,
            scratch_shapes=[dma((16 + n_ex,))],
            compiler_params=pltpu.CompilerParams(vmem_limit_bytes=16 * 2**20),
            name="finish",
        )(expert_slot, *out)
        return (*state, jnp.transpose(placed, (0, 2, 1)), server_key)

    return jax.shard_map(
        on_device,
        mesh=mesh,
        in_specs=(
            P("dp", "expert", None, None),
            P("dp", None, "expert"),
            P("expert", "dp", None),
            P("expert", "dp", None),
            P("expert", "dp", None),
            P("dp", "expert"),
            P("dp", "expert"),
            P("dp", "expert"),
            P(),
            P(None, "expert"),
            P(),
            P(),
        ),
        out_specs=(
            P("expert", "dp", None),
            P("expert", "dp", None),
            P("expert", "dp", None),
            P("dp", "expert"),
            P("dp", "expert"),
            P("dp", "expert"),
            P(None, "expert", "dp"),
            P("expert", None),
        ),
        check_vma=False,
    )
```

```python
import functools
import math

import jax
import jax.numpy as jnp
from jax import lax
from jax.experimental import pallas as pl
from jax.experimental.pallas import tpu as pltpu
from jax.sharding import PartitionSpec as P

HD = 128
BLOCK = 128
BETA_ONE = 0.9
BETA_TWO = 0.95
LEARN = 0.01
DECAY = 0.1
EPSILON = 1e-08
LIMIT = 448.0
CORRECT_ONE = 1.0 - 0.9**10
CORRECT_TWO = 1.0 - 0.95**10
MESH = pl.DeviceIdType.MESH
F32 = jnp.float32
BF16 = jnp.bfloat16


def adam_update(param, moment, second, grad):
    moment = BETA_ONE * moment + (1.0 - BETA_ONE) * grad
    second = BETA_TWO * second + (1.0 - BETA_TWO) * grad * grad
    scaled = moment * (1.0 / CORRECT_ONE)
    corrected = scaled / (jnp.sqrt(second * (1.0 / CORRECT_TWO)) + EPSILON)
    return (param * (1.0 - LEARN * DECAY) - LEARN * corrected, moment, second)


def loop(count, body):
    def step(i, carry):
        body(i)
        return carry

    lax.fori_loop(0, count, step, 0)


def dest_of(z, n_ex, t):
    if n_ex != 4:
        return (z + n_ex - 1 - t) % n_ex
    side = z // 2
    near = z + side * (3 - 2 * z)
    dest = (3, 2 - 2 * near, 1 + near, near)[t]
    return dest + side * (3 - 2 * dest)


def plan(n_ex, cw):
    units = []
    for t in range(n_ex):
        wide = min(cw, 2 * BLOCK)
        sizes = [wide] * (cw // wide)
        if wide > BLOCK and t == 0:
            sizes[:1] = [BLOCK, wide - BLOCK]
        if wide > BLOCK and t == n_ex - 1:
            sizes[-1:] = [wide - BLOCK, BLOCK]
        at = 0
        for size in sizes:
            units.append((t, at, size))
            at += size
    units.insert(2, None)
    return units


def kernel(
    n_dp,
    n_ex,
    eg_hbm,
    kg_hbm,
    ep_hbm,
    em_hbm,
    es_hbm,
    kp_hbm,
    km_hbm,
    ks_hbm,
    e_scale_hbm,
    k_scale_hbm,
    order_hbm,
    o_ep,
    o_em,
    o_es,
    o_kp,
    o_km,
    o_ks,
    o_arr,
    o_key,
    k_gath,
    e_scale,
    k_scale,
    order,
    *rest,
):
    chips = n_dp // 2
    m = chips.bit_length() - 1
    load_sem, s0_sem, rs_sem, a2a_sem, ag_sem, pair_sem, small_sem, arrive_sem, ready = rest[:9]
    rest = list(rest[9:])

    d = lax.axis_index("dp")
    z = lax.axis_index("expert")
    core = d % 2
    chip = d // 2
    bits = [(chip // 2**i) % 2 for i in range(m)]

    def chip_of(values):
        total = values[0] * 1
        for i in range(1, m):
            total = total + values[i] * 2**i
        return total

    def partner(i):
        return d + (1 - 2 * bits[i]) * 2 ** (i + 1)

    other_core = d + 1 - 2 * core
    orders = (list(range(m)), list(range(m))[::-1])

    rows, width = ep_hbm.shape[1:]
    krows, kwidth = kp_hbm.shape
    cw = width // n_ex
    layout = plan(n_ex, cw)

    class Unit:
        pass

    units = []
    for u, entry in enumerate(layout):
        w = Unit()
        w.u = u
        w.key = entry is None
        w.far, w.own, w.s0s, w.s0r = (rest.pop(0) for _ in range(4))
        w.snd = [rest.pop(0) for _ in range(m)]
        w.rcv = [rest.pop(0) for _ in range(m)]
        if w.key:
            w.rows, w.cols = krows, kwidth
            w.columns = pl.ds(0, kwidth)
            w.grad = kg_hbm
            w.state = [o_kp, o_km, o_ks]
            w.state_in = [kp_hbm, km_hbm, ks_hbm]
        else:
            t, w.at, w.cols = entry
            w.rows = rows
            w.dest = dest_of(z, n_ex, t)
            w.mine = t == n_ex - 1
            w.columns = pl.ds(pl.multiple_of(w.dest * cw + w.at, BLOCK), w.cols)
            w.grad = eg_hbm
            w.state = [r.at[0, :, w.columns] for r in (o_ep, o_em, o_es)]
            w.state_in = [r.at[0, :, w.columns] for r in (ep_hbm, em_hbm, es_hbm)]
            if not w.mine:
                w.grid = rest.pop(0)
                w.exchange = pltpu.make_async_remote_copy(
                    src_ref=w.grid,
                    dst_ref=o_arr.at[z, :, pl.ds(w.at, w.cols)],
                    send_sem=a2a_sem.at[u],
                    recv_sem=arrive_sem.at[z],
                    device_id=(d, w.dest),
                    device_id_type=MESH,
                )
        w.half = w.rows // 2
        w.load_far = pltpu.make_async_copy(
            w.grad.at[:, 1 - core, :, w.columns], w.far, load_sem.at[u, 0]
        )
        w.load_own = pltpu.make_async_copy(
            w.grad.at[:, core, :, w.columns], w.own, load_sem.at[u, 1]
        )
        w.load_state = [
            pltpu.make_async_copy(w.state_in[i], w.state[i], load_sem.at[u, 2 + i])
            for i in range(3)
        ]
        w.s0 = pltpu.make_async_remote_copy(
            src_ref=w.s0s,
            dst_ref=w.s0r,
            send_sem=s0_sem.at[u, 0],
            recv_sem=s0_sem.at[u, 1],
            device_id=(other_core, z),
            device_id_type=MESH,
        )
        w.rs = [
            [
                pltpu.make_async_remote_copy(
                    src_ref=w.snd[s].at[h],
                    dst_ref=w.rcv[s].at[h],
                    send_sem=rs_sem.at[u, s, h, 0],
                    recv_sem=rs_sem.at[u, s, h, 1],
                    device_id=(partner(orders[h][s]), z),
                    device_id_type=MESH,
                )
                for h in range(2)
            ]
            for s in range(m)
        ]
        units.append(w)

    small = [
        pltpu.make_async_copy(source, target, small_sem.at[i])
        for i, (source, target) in enumerate(
            ((k_scale_hbm, k_scale), (e_scale_hbm, e_scale), (order_hbm, order))
        )
    ]
    def load(u):
        if 0 <= u < len(units):
            units[u].load_far.start()
            units[u].load_own.start()

    def load_state(u):
        if 0 <= u < len(units):
            for c in units[u].load_state:
                c.start()

    barrier = pltpu.get_barrier_semaphore()
    for k in range(1, chips):
        pl.semaphore_signal(
            barrier, inc=1, device_id=((chip + k) % chips * 2, z), device_id_type=MESH
        )

    @pl.when(core == 1)
    def _():
        pl.semaphore_signal(barrier, inc=1, device_id=(other_core, z), device_id_type=MESH)

    def plane_ready():
        @pl.when(core == 0)
        def _():
            pl.semaphore_wait(barrier, 2 * chips - 1)
            pl.semaphore_signal(
                ready.at[0], inc=1, device_id=(other_core, z), device_id_type=MESH
            )

        @pl.when(core == 1)
        def _():
            pl.semaphore_wait(ready.at[0], 1)
            for k in range(1, n_ex):
                pl.semaphore_signal(
                    barrier, inc=1, device_id=(d, (z + k) % n_ex), device_id_type=MESH
                )

    def planes_ready():
        @pl.when(core == 1)
        def _():
            pl.semaphore_wait(barrier, n_ex - 1)
            pl.semaphore_signal(
                ready.at[1], inc=1, device_id=(other_core, z), device_id_type=MESH
            )

        @pl.when(core == 0)
        def _():
            pl.semaphore_wait(ready.at[1], 1)

    load(0)
    load(1)

    def index_in(values, h, s):
        total = 0
        for k, b in enumerate(orders[h][s + 1 :]):
            total = total + values[b] * 2**k
        return total

    def rows_at(i, step):
        return pl.ds(pl.multiple_of(i * step, step), step)

    def rows_in(w, h, i, step):
        return pl.ds(pl.multiple_of(h * w.half + i * step, step), step)

    def block_sum(w, values, h, s, i, step):
        q = chip_of(values)
        r, whole = rows_at(i, step), rows_in(w, h, i, step)
        total = w.own[q, whole, :] + w.s0r[q, whole, :].astype(F32)
        for past in range(s):
            total = total + w.rcv[past][h, index_in(values, h, past), r, :].astype(F32)
        return total

    def first(w):
        w.load_far.wait()
        step = math.gcd(w.rows, 16384 // w.cols)
        per = w.rows // step

        def body(i):
            q = i // per
            r = pl.ds(pl.multiple_of((i % per) * step, step), step)
            w.s0s[q, r, :] = w.far[q, r, :].astype(BF16)

        loop(chips * per, body)
        if w.u == 0:
            plane_ready()
        w.s0.start()

    def reduce(w, s):
        if s == 0:
            w.load_own.wait()
            w.s0.wait_recv()
        step = math.gcd(w.half, 16384 // w.cols)
        for h in range(2):
            if s > 0:
                w.rs[s - 1][h].wait_recv()
            left = orders[h][s + 1 :]
            for slot in range(2 ** len(left)):
                values = list(bits)
                values[orders[h][s]] = 1 - bits[orders[h][s]]
                for k, b in enumerate(left):
                    values[b] = (slot >> k) & 1

                def body(i):
                    total = block_sum(w, values, h, s, i, step)
                    w.snd[s][h, slot, rows_at(i, step), :] = total.astype(BF16)

                loop(w.half // step, body)
            w.rs[s][h].start()

    def update(w):
        for c in w.load_state:
            c.wait()
        if w.u == 0:
            for c in small:
                c.wait()
        step = math.gcd(w.half, max(16, 8192 // w.cols))
        for h in range(2):
            w.rs[m - 1][h].wait_recv()

            def body(i):
                r = rows_in(w, h, i, step)
                grad = block_sum(w, bits, h, m, i, step)
                new = adam_update(*(ref[r, :] for ref in w.state), grad)
                for ref, value in zip(w.state, new):
                    ref[r, :] = value
                block = (d * w.rows + h * w.half + i * step) // BLOCK
                for j in range(w.cols // BLOCK):
                    if w.key:
                        scale = k_scale[block, j]
                    else:
                        scale = e_scale[block, z, w.dest * (cw // BLOCK) + w.at // BLOCK + j]
                    cols = slice(j * BLOCK, (j + 1) * BLOCK)
                    part = jnp.clip(new[0][:, cols] / scale, -LIMIT, LIMIT).astype(BF16)
                    if w.key:
                        k_gath[chip, core, r, cols] = part
                    elif w.mine:
                        o_arr[z, r, w.at + j * BLOCK : w.at + (j + 1) * BLOCK] = part
                    else:
                        w.grid[r, cols] = part

            loop(w.half // step, body)
        if w.key:
            gather_send(0)
        elif not w.mine:
            if w.u == 0:
                planes_ready()
            w.exchange.start()
        w.s0.wait_send()
        for s in range(m):
            for h in range(2):
                w.rs[s][h].wait_send()

    khalf = kwidth // 2

    def gather_copies(s):
        copies = []
        for h in range(2):
            done = orders[h][:s]
            for slot in range(2**s):
                values = list(bits)
                for k, b in enumerate(done):
                    values[b] = (slot >> k) & 1
                ref = k_gath.at[chip_of(values), core, :, pl.ds(h * khalf, khalf)]
                copies.append(
                    pltpu.make_async_remote_copy(
                        src_ref=ref,
                        dst_ref=ref,
                        send_sem=ag_sem.at[s, h, slot, 0],
                        recv_sem=ag_sem.at[s, h, slot, 1],
                        device_id=(partner(orders[h][s]), z),
                        device_id_type=MESH,
                    )
                )
        return copies

    pair = pltpu.make_async_remote_copy(
        src_ref=k_gath.at[:, core],
        dst_ref=k_gath.at[:, core],
        send_sem=pair_sem.at[0],
        recv_sem=pair_sem.at[1],
        device_id=(other_core, z),
        device_id_type=MESH,
    )

    def gather_send(s):
        for c in gather_copies(s):
            c.start()

    def gather_next(s):
        for c in gather_copies(s):
            c.wait_recv()
        if s + 1 < m:
            gather_send(s + 1)
        else:
            pair.start()

    def key_finish():
        pair.wait_recv()
        source = lax.broadcasted_iota(jnp.int32, (HD, HD), 0)
        pick = jnp.where(source == order[...], 1.0, 0.0).astype(BF16)
        span = HD // (2 * krows)
        wide = 256
        for head in range(o_key.shape[1] // HD):
            for j in range(kwidth // wide):
                cols = slice(j * wide, (j + 1) * wide)
                block = k_gath[head * span : (head + 1) * span, :, :, cols].reshape(HD, wide)
                turned = lax.dot_general(
                    block, pick, (((0,), (0,)), ((), ())), preferred_element_type=F32
                )
                o_key[cols, head * HD : (head + 1) * HD] = turned.astype(BF16)

    stages = [first] + [functools.partial(reduce, s=s) for s in range(m)] + [update]
    lags = [0, 1] + [1 + 2 * s for s in range(1, m)] + [2 * m]
    last = len(units) - 1
    for slot in range(len(units) + lags[-1]):
        for s, (stage, lag) in enumerate(zip(stages, lags)):
            if 0 <= slot - lag <= last:
                stage(units[slot - lag])
            if s == 0:
                load(slot + 2)
                load_state(slot)
                if slot == 0:
                    for c in small:
                        c.start()
            if s == m and slot - lag == last - 1:
                key_finish()
        step = slot - lags[-1] - 1 - layout.index(None)
        if 0 <= step < m:
            gather_next(step)

    for k in range(1, n_ex):
        source = (z + k) % n_ex
        pltpu.make_async_remote_copy(
            src_ref=o_arr.at[source],
            dst_ref=o_arr.at[source],
            send_sem=a2a_sem.at[0],
            recv_sem=arrive_sem.at[source],
            device_id=(d, source),
            device_id_type=MESH,
        ).wait_recv()
    for w in units:
        if not w.key and not w.mine:
            w.exchange.wait_send()
    for s in range(m):
        for c in gather_copies(s):
            c.wait_send()
    pair.wait_send()


def finish(n_ex, slot, *refs):
    sources, targets, sems = refs[:8], refs[8:16], refs[16]
    pairs = []
    for i in range(3):
        part = sources[i].shape[1] // 4
        for k in range(4):
            at = pl.ds(k * part, part)
            pairs.append((sources[i].at[:, at], targets[i].at[:, at]))
    for i in (7, 3, 4, 5):
        pairs.append((sources[i], targets[i]))
    for e in range(n_ex):
        pairs.append((sources[6].at[e], targets[6].at[slot[e]]))
    copies = [pltpu.make_async_copy(a, b, sems.at[i]) for i, (a, b) in enumerate(pairs)]
    for c in copies:
        c.start()
    for c in copies:
        c.wait()


def solution(mesh):
    n_dp, n_ex = mesh.shape["dp"], mesh.shape["expert"]

    def on_device(
        expert_partials,
        key_partials,
        expert_param,
        expert_moment,
        expert_second,
        key_param,
        key_moment,
        key_second,
        expert_scales,
        key_scales,
        rotary_order,
        expert_slot,
    ):
        chips = n_dp // 2
        m = chips.bit_length() - 1
        _, rows, width = expert_param.shape
        krows, kwidth = key_param.shape
        key_rows = key_partials.shape[1]
        cw = width // n_ex
        layout = plan(n_ex, cw)
        eg = expert_partials.reshape(chips, 2, rows, width)
        kg = key_partials.reshape(chips, 2, krows, kwidth)
        shape = jax.ShapeDtypeStruct
        anywhere = pl.BlockSpec(memory_space=pl.ANY)
        hbm = pl.BlockSpec(memory_space=pltpu.HBM)
        scalars = pl.BlockSpec(memory_space=pltpu.SMEM)
        vector = pl.BlockSpec(memory_space=pltpu.VMEM)
        dma = pltpu.SemaphoreType.DMA
        buffers = []
        for entry in layout:
            high, wide = (krows, kwidth) if entry is None else (rows, entry[2])
            buffers += [pltpu.VMEM((chips, high, wide), t) for t in (F32, F32, BF16, BF16)]
            steps = [
                pltpu.VMEM((2, 2 ** (m - 1 - s), high // 2, wide), BF16) for s in range(m)
            ]
            buffers += steps + steps
            if entry is not None and entry[0] < n_ex - 1:
                buffers.append(pltpu.VMEM((high, wide), BF16))
        here = functools.partial(pltpu.with_memory_space_constraint, memory_space=pltpu.HBM)
        out = pl.pallas_call(
            functools.partial(kernel, n_dp, n_ex),
            out_shape=[shape(expert_param.shape, F32)] * 3
            + [shape(key_param.shape, F32)] * 3
            + [shape((n_ex, rows, cw), BF16), shape((kwidth, key_rows), BF16)],
            in_specs=[hbm] * 11,
            out_specs=[vector] * 8,
            scratch_shapes=[
                pltpu.VMEM((chips, 2, krows, kwidth), BF16),
                pltpu.SMEM(expert_scales.shape[1:2] + (n_ex,) + expert_scales.shape[2:], F32),
                pltpu.SMEM(key_scales.shape, F32),
                pltpu.VMEM((1, HD), jnp.int32),
                dma((len(layout), 5)),
                dma((len(layout), 2)),
                dma((len(layout), m, 2, 2)),
                dma((len(layout),)),
                dma((m, 2, 2 ** (m - 1), 2)),
                dma((2,)),
                dma((3,)),
                dma((n_ex,)),
                pltpu.SemaphoreType.REGULAR((2,)),
            ]
            + buffers,
            compiler_params=pltpu.CompilerParams(
                collective_id=0, has_side_effects=True, vmem_limit_bytes=int(46 * 2**20)
            ),
            name="reduce_update_exchange",
        )(
            *map(
                here,
                (
                    eg,
                    kg,
                    expert_param,
                    expert_moment,
                    expert_second,
                    key_param,
                    key_moment,
                    key_second,
                    jnp.transpose(expert_scales, (1, 0, 2)),
                    key_scales,
                    rotary_order.reshape(1, HD),
                ),
            )
        )
        *state, placed, server_key = pl.pallas_call(
            functools.partial(finish, n_ex),
            out_shape=[shape(x.shape, x.dtype) for x in out],
            in_specs=[scalars] + [vector] * 8,
            out_specs=[anywhere] * 8,
            scratch_shapes=[dma((16 + n_ex,))],
            compiler_params=pltpu.CompilerParams(vmem_limit_bytes=16 * 2**20),
            name="finish",
        )(expert_slot, *out)
        return (*state, jnp.transpose(placed, (0, 2, 1)), server_key)

    return jax.shard_map(
        on_device,
        mesh=mesh,
        in_specs=(
            P("dp", "expert", None, None),
            P("dp", None, "expert"),
            P("expert", "dp", None),
            P("expert", "dp", None),
            P("expert", "dp", None),
            P("dp", "expert"),
            P("dp", "expert"),
            P("dp", "expert"),
            P(),
            P(None, "expert"),
            P(),
            P(),
        ),
        out_specs=(
            P("expert", "dp", None),
            P("expert", "dp", None),
            P("expert", "dp", None),
            P("dp", "expert"),
            P("dp", "expert"),
            P("dp", "expert"),
            P(None, "expert", "dp"),
            P("expert", None),
        ),
        check_vma=False,
    )
```
